32 devices in a mesh: rep: 2 (over y), cell: 4 (over z), scen: 4 (over x, core).
Axes of the slice: x: 2, y: 2, z: 4, core: 2. Of those that a mesh axis runs over, the one named last changes fastest.
Arguments:
- hydrograph: bfloat16 [1024, 128], P(('rep', 'scen')), parts along dimension 0, may hold values from -6 to 6
- scen_group: int32 [1024], P(('rep', 'scen')), parts along dimension 0, may hold values from 0 to 15
- cell_feat: bfloat16 [4096, 128], P(('rep', 'cell')), parts along dimension 0, may hold values from -6 to 6
- cell_class: int32 [32], P(('rep', 'cell')), parts along dimension 0, may hold values from 0 to 15
- branch_in: bfloat16 [128, 1024], replicated, may hold values from -0.5 to 0.5
- group_table: bfloat16 [16, 1024], replicated, may hold values from -3 to 3
- branch_out: bfloat16 [1024, 512], replicated, may hold values from -0.1875 to 0.1875
- trunk_in: bfloat16 [128, 512], replicated, may hold values from -0.5 to 0.5
- class_table: bfloat16 [16, 512], replicated, may hold values from -3 to 3
- trunk_out: bfloat16 [512, 512], replicated, may hold values from -0.25 to 0.25
- targets: float32 [1024, 2048], P(('rep', 'scen'), 'cell'), parts along dimension 0, may hold values from -6 to 6
Outputs:
- gradient: float32 [2015232], P(('rep', 'cell', 'scen')), parts along dimension 0
The draws below stay inside these ranges and needn't reach their ends.
There are 2 independent parts, one for each index of `rep`. The reference program is written for one: setup_inputs(seed, part) draws one part's arguments, and reference() takes and returns one part's arrays. A program takes and returns all parts, laid end to end along the dimension named above; an argument that names none is the same for every part. Nothing has to cross between parts.
All inputs are finite; a program needn't handle non-finite values.
Results may differ from the reference program's by a relative error of at most 0.0034.
Values may be sent and summed in bfloat16 or wider, within the bound.
A program may use at most 64 MiB of HBM per device.

```python
import jax
import jax.numpy as jnp
from jax import lax

SAMPLES = 128
BWIDTH = 1024
BASIS = 512
FEATS = 128
TWIDTH = 512
GROUPS = 16
CLASSES = 16
SCEN = 512
CELLS = 2048


def set_ends(array, own_key, low, top_value):
    index_at = [jax.random.randint(jax.random.fold_in(own_key, axis), (), 0, length) for axis, length in enumerate(array.shape)]
    widest = array.shape.index(max(array.shape))
    next_to = index_at[:widest] + [(index_at[widest] + 1) % array.shape[widest]] + index_at[widest + 1:]
    return array.at[tuple(index_at)].set(low).at[tuple(next_to)].set(top_value)


def block_scale(own_key, shape, split, smallest, largest):
    def one(dim, parts):
        draws = jax.random.uniform(jax.random.fold_in(jax.random.fold_in(own_key, 6), dim), (parts,), jnp.float32, smallest / len(split), largest / len(split))
        return jnp.repeat(jnp.exp(draws), shape[dim] // parts).reshape((-1,) + (1,) * (len(shape) - dim - 1))

    loudness = one(*split[0])
    for cut in split[1:]:
        loudness = loudness * one(*cut)
    return loudness


def noise(key, shape, deviation, reach, pieces=(), held_as=jnp.bfloat16):
    gain = block_scale(key, shape, pieces, -0.22, 0.18) if pieces else 1.0
    array = jax.random.normal(key, shape, jnp.float32) * deviation * gain
    return jnp.minimum(jnp.maximum(array, -reach), reach).astype(held_as)


def setup_inputs(seed: int = 0, part: int = 0) -> dict:
    arg_keys = jax.random.split(jax.random.key(seed), 12)
    part_keys = jax.random.split(jax.random.fold_in(arg_keys[11], part), 12)
    return {
        "hydrograph": noise(part_keys[0], (SCEN, SAMPLES), 1.0, 6.0, ((0, 4),)),
        "scen_group": set_ends(jax.random.randint(part_keys[1], (SCEN,), 0, GROUPS), jax.random.fold_in(part_keys[1], 1), 0, GROUPS - 1).astype(jnp.int32),
        "cell_feat": noise(part_keys[2], (CELLS, FEATS), 1.0, 6.0, ((0, 4),)),
        "cell_class": set_ends(jax.random.randint(part_keys[3], (CELLS // 128,), 0, CLASSES), jax.random.fold_in(part_keys[3], 1), 0, CLASSES - 1).astype(jnp.int32),
        "branch_in": noise(arg_keys[4], (SAMPLES, BWIDTH), SAMPLES ** -0.5, 0.5),
        "group_table": noise(arg_keys[5], (GROUPS, BWIDTH), 0.5, 3.0),
        "branch_out": noise(arg_keys[6], (BWIDTH, BASIS), BWIDTH ** -0.5, 0.1875),
        "trunk_in": noise(arg_keys[7], (FEATS, TWIDTH), FEATS ** -0.5, 0.5),
        "class_table": noise(arg_keys[8], (CLASSES, TWIDTH), 0.5, 3.0),
        "trunk_out": noise(arg_keys[9], (TWIDTH, BASIS), TWIDTH ** -0.5, 0.25),
        "targets": noise(part_keys[10], (SCEN, CELLS), 1.0, 6.0, ((0, 4), (1, 4)), jnp.float32),
    }


def contract(left, right, left_dim, right_dim):
    return lax.dot_general(left, right, (((left_dim,), (right_dim,)), ((), ())), preferred_element_type=jnp.float32)

def reference(hydrograph, scen_group, cell_feat, cell_class, branch_in, group_table, branch_out, trunk_in, class_table, trunk_out, targets):
    group_hot = (scen_group[:, None] == jnp.arange(GROUPS, dtype=jnp.int32)[None, :]).astype(jnp.bfloat16)
    class_cells = jnp.repeat(cell_class, 128)
    class_hot = (class_cells[:, None] == jnp.arange(CLASSES, dtype=jnp.int32)[None, :]).astype(jnp.bfloat16)
    pre_branch = jnp.dot(hydrograph, branch_in, preferred_element_type=jnp.float32) + jnp.dot(group_hot, group_table, preferred_element_type=jnp.float32)
    hid_branch = jax.nn.gelu(pre_branch).astype(jnp.bfloat16)
    coeff = jnp.dot(hid_branch, branch_out, preferred_element_type=jnp.float32).astype(jnp.bfloat16)
    pre_trunk = jnp.dot(cell_feat, trunk_in, preferred_element_type=jnp.float32) + jnp.dot(class_hot, class_table, preferred_element_type=jnp.float32)
    hid_trunk = jnp.tanh(pre_trunk).astype(jnp.bfloat16)
    basis = jnp.dot(hid_trunk, trunk_out, preferred_element_type=jnp.float32).astype(jnp.bfloat16)
    predicted = contract(coeff, basis, 1, 1) * (1.0 / jnp.sqrt(jnp.float32(BASIS)))
    resid = ((predicted - targets) * (1.0 / jnp.sqrt(jnp.float32(SCEN) * jnp.float32(CELLS)))).astype(jnp.bfloat16)
    d_coeff = jnp.dot(resid, basis, preferred_element_type=jnp.float32).astype(jnp.bfloat16)
    d_basis = contract(resid, coeff, 0, 0).astype(jnp.bfloat16)
    g_branch_out = contract(hid_branch, d_coeff, 0, 0)
    d_hid_branch = contract(d_coeff, branch_out, 1, 1)
    d_pre_branch = jax.vjp(jax.nn.gelu, pre_branch)[1](d_hid_branch)[0].astype(jnp.bfloat16)
    g_branch_in = contract(hydrograph, d_pre_branch, 0, 0)
    g_group_table = contract(group_hot, d_pre_branch, 0, 0)
    g_trunk_out = contract(hid_trunk, d_basis, 0, 0)
    d_hid_trunk = contract(d_basis, trunk_out, 1, 1)
    d_pre_trunk = jax.vjp(jnp.tanh, pre_trunk)[1](d_hid_trunk)[0].astype(jnp.bfloat16)
    g_trunk_in = contract(cell_feat, d_pre_trunk, 0, 0)
    g_class_table = contract(class_hot, d_pre_trunk, 0, 0)
    return jnp.concatenate([g_branch_in.ravel(), g_group_table.ravel(), g_branch_out.ravel(), g_trunk_in.ravel(), g_class_table.ravel(), g_trunk_out.ravel()])
```

```python
import math

import jax
import jax.numpy as jnp
from jax import lax
from jax.experimental import pallas as pl
from jax.experimental.pallas import tpu as pltpu
from jax.sharding import PartitionSpec as P

MESH = pl.DeviceIdType.MESH
BF16 = jnp.bfloat16
F32 = jnp.float32
WIDE = 512


def contract(left, right, left_dim, right_dim):
    return lax.dot_general(
        left, right, (((left_dim,), (right_dim,)), ((), ())), preferred_element_type=jnp.float32
    )


def plain_shards(
    hydrograph,
    scen_group,
    cell_feat,
    cell_class,
    branch_in,
    group_table,
    branch_out,
    trunk_in,
    class_table,
    trunk_out,
    targets,
):
    cell_count = lax.axis_size("cell")
    scen_count = lax.axis_size("scen")
    whole_pairs = jnp.float32(hydrograph.shape[0] * scen_count) * jnp.float32(
        cell_feat.shape[0] * cell_count
    )
    group_hot = (
        scen_group[:, None] == jnp.arange(group_table.shape[0], dtype=jnp.int32)[None, :]
    ).astype(BF16)
    class_cells = jnp.repeat(cell_class, 128)
    class_hot = (
        class_cells[:, None] == jnp.arange(class_table.shape[0], dtype=jnp.int32)[None, :]
    ).astype(BF16)
    pre_branch = contract(hydrograph, branch_in, 1, 0) + contract(group_hot, group_table, 1, 0)
    hid_branch = jax.nn.gelu(pre_branch).astype(BF16)
    coeff_local = contract(hid_branch, branch_out, 1, 0).astype(BF16)
    pre_trunk = contract(cell_feat, trunk_in, 1, 0) + contract(class_hot, class_table, 1, 0)
    hid_trunk = jnp.tanh(pre_trunk).astype(BF16)
    basis_local = contract(hid_trunk, trunk_out, 1, 0).astype(BF16)
    predicted = contract(coeff_local, basis_local, 1, 1) * (
        1.0 / jnp.sqrt(jnp.float32(branch_out.shape[1]))
    )
    resid = ((predicted - targets) * (1.0 / jnp.sqrt(whole_pairs))).astype(BF16)
    d_coeff = lax.psum(contract(resid, basis_local, 1, 0), "cell").astype(BF16)
    d_basis = lax.psum(contract(resid, coeff_local, 0, 0).astype(BF16), "scen")
    g_branch_out = contract(hid_branch, d_coeff, 0, 0)
    d_hid_branch = contract(d_coeff, branch_out, 1, 1)
    d_pre_branch = jax.vjp(jax.nn.gelu, pre_branch)[1](d_hid_branch)[0].astype(BF16)
    g_branch_in = contract(hydrograph, d_pre_branch, 0, 0)
    g_group_table = contract(group_hot, d_pre_branch, 0, 0)
    g_trunk_out = contract(hid_trunk, d_basis, 0, 0)
    d_hid_trunk = contract(d_basis, trunk_out, 1, 1)
    d_pre_trunk = jax.vjp(jnp.tanh, pre_trunk)[1](d_hid_trunk)[0].astype(BF16)
    g_trunk_in = contract(cell_feat, d_pre_trunk, 0, 0)
    g_class_table = contract(class_hot, d_pre_trunk, 0, 0)
    branch_flat = jnp.concatenate(
        [g_branch_in.ravel(), g_group_table.ravel(), g_branch_out.ravel()]
    )
    trunk_flat = jnp.concatenate([g_trunk_in.ravel(), g_class_table.ravel(), g_trunk_out.ravel()])
    branch_flat = branch_flat * (lax.axis_index("cell") == 0).astype(F32)
    trunk_flat = trunk_flat * (lax.axis_index("scen") == 0).astype(F32)
    flat_grad = jnp.concatenate([branch_flat, trunk_flat])
    return lax.psum_scatter(flat_grad, ("cell", "scen"), scatter_dimension=0, tiled=True)


def choose(rows, cols, first, scale, offset):
    row = lax.broadcasted_iota(jnp.int32, (rows, cols), 0) + first
    col = lax.broadcasted_iota(jnp.int32, (rows, cols), 1) * scale + offset
    return (row == col).astype(F32).astype(BF16)


def make_kernel(cells, scens, scen_rows, cell_rows, bwidth, twidth, groups, classes, samples, feats,
                own_rows, pairs):
    pad_rows = -(-own_rows // 16) * 16
    chunk = scen_rows // cells
    in_rows = 2 * (samples + groups)
    branch_rows = in_rows + bwidth
    trunk_lead = feats + classes
    all_scen = scens * scen_rows
    inv_root = 1.0 / math.sqrt(WIDE)
    inv_pairs = 1.0 / math.sqrt(pairs)
    trunk_dests = [
        d for d in range(cells) if ((d + 1) * scens) * own_rows > branch_rows
    ]
    tile = 128

    def kernel(hydro, group, feat, klass, b_in, g_tab, b_out, t_in, c_tab, t_out, targets, out,
               x_all, w_b, w_t, x_t, dgelu, hid, coeff, hid_t, basis, resid, part_f, part_b,
               part_in, dc, dbasis, dpre_t, pick_in0, pick_in1, pick_hid, t_own, t_send, t_recv,
               dpre_b, total,
               x_ss, x_rs, r_ss, r_rs, p_ss, p_rs, z_ss, z_rs, d_ss, d_rs, t_ss, t_rs):
        c = lax.axis_index("cell")
        s = lax.axis_index("scen")
        first = (c * scens + s) * own_rows

        def scen_at(k):
            return lax.rem(s + k, scens)

        def cell_at(k):
            return lax.rem(c + k, cells)

        def to_scen(src, dst, ss, rs, k):
            return pltpu.make_async_remote_copy(
                src_ref=src, dst_ref=dst, send_sem=ss.at[k - 1], recv_sem=rs.at[k - 1],
                device_id={"scen": scen_at(k)}, device_id_type=MESH)

        def to_cell(src, dst, ss, rs, k):
            return pltpu.make_async_remote_copy(
                src_ref=src, dst_ref=dst, send_sem=ss.at[k - 1], recv_sem=rs.at[k - 1],
                device_id={"cell": cell_at(k)}, device_id_type=MESH)

        barrier = pltpu.get_barrier_semaphore()
        for k in range(1, scens):
            pl.semaphore_signal(barrier, inc=1, device_id={"scen": scen_at(k)}, device_id_type=MESH)
        for k in range(1, cells):
            pl.semaphore_signal(barrier, inc=1, device_id={"cell": cell_at(k)}, device_id_type=MESH)

        hot = (lax.broadcasted_iota(jnp.int32, (128, scen_rows), 0) == group[...]).astype(F32)
        x_all[s, :, 0:samples] = hydro[...]
        x_all[s, :, samples:samples + 128] = hot.T.astype(BF16)
        pl.semaphore_wait(barrier, scens + cells - 2)
        x_copies = [to_scen(x_all.at[s], x_all.at[s], x_ss, x_rs, k) for k in range(1, scens)]
        for copy in x_copies:
            copy.start()

        w_b[0:samples, :] = b_in[...]
        w_b[samples:samples + groups, :] = g_tab[...]
        w_b[samples + groups:, :] = jnp.zeros((128 - groups, bwidth), BF16)
        w_t[0:feats, :] = t_in[...]
        w_t[feats:feats + classes, :] = c_tab[...]
        w_t[feats + classes:, :] = jnp.zeros((128 - classes, twidth), BF16)

        def branch(p):
            pre = contract(x_all[p], w_b[...], 1, 0)
            inner = math.sqrt(2.0 / math.pi)
            bent = jnp.tanh(inner * (pre + 0.044715 * (pre * pre * pre)))
            cdf = 0.5 * (1.0 + bent)
            hid[p] = (pre * cdf).astype(BF16)
            dgelu[p] = cdf + (0.5 * inner) * pre * (1.0 - bent * bent) * (
                1.0 + (3.0 * 0.044715) * (pre * pre))
            coeff[p] = contract(hid[p], b_out[...], 1, 0).astype(BF16)

        branch(s)

        @pl.loop(0, cell_rows // tile)
        def _(b):
            rows = pl.ds(pl.multiple_of(b * tile, tile), tile)
            x_t[rows, 0:feats] = feat[rows, :]
            lane = lax.broadcasted_iota(jnp.int32, (tile, 128), 1)
            x_t[rows, feats:feats + 128] = (lane == klass[b]).astype(F32).astype(BF16)
            pre = contract(x_t[rows, :], w_t[...], 1, 0)
            hid_t[rows, :] = jnp.tanh(pre).astype(BF16)
            basis[rows, :] = contract(hid_t[rows, :], t_out[...], 1, 0).astype(BF16)

        predicted = contract(coeff[s], basis[...], 1, 1) * inv_root
        resid[s] = ((predicted - targets[...]) * inv_pairs).astype(BF16)
        r_copies = [to_scen(resid.at[s], resid.at[s], r_ss, r_rs, k) for k in range(1, scens)]
        for copy in r_copies:
            copy.start()
        partial = contract(resid[s], basis[...], 1, 0)
        for d in range(cells):
            part_f[d] = partial[d * chunk:(d + 1) * chunk]
            part_b[d] = partial[d * chunk:(d + 1) * chunk].astype(BF16)
        p_copies = [to_cell(part_b.at[cell_at(k)], part_in.at[k - 1], p_ss, p_rs, k)
                    for k in range(1, cells)]
        for copy in p_copies:
            copy.start()

        for copy in x_copies:
            copy.wait()
        @pl.loop(1, scens)
        def _(k):
            branch(lax.rem(s + k, scens))

        for copy in p_copies:
            copy.wait()
        summed = part_f[c]
        for k in range(cells - 1):
            summed = summed + part_in[k].astype(F32)
        dc[s, c] = summed.astype(BF16)
        z_copies = [to_cell(dc.at[s, c], dc.at[s, c], z_ss, z_rs, k) for k in range(1, cells)]
        for copy in z_copies:
            copy.start()

        for copy in r_copies:
            copy.wait()
        @pl.loop(0, cell_rows // tile)
        def _(b):
            cols = pl.ds(pl.multiple_of(b * tile, tile), tile)
            sums = jnp.zeros((tile, WIDE), F32)
            for p in range(scens):
                sums = sums + contract(resid[p, :, cols], coeff[p], 0, 0)
            dbasis[cols, :] = sums.astype(BF16)

        def trunk_need(d, me):
            return (d * scens + me + 1) * own_rows > branch_rows

        def lead_need(d, me):
            return ((d * scens + me + 1) * own_rows > branch_rows) & (
                (d * scens + me) * own_rows < branch_rows + trunk_lead)

        lead_any = lead_need(trunk_dests[0], s)
        for d in trunk_dests[1:]:
            lead_any = lead_any | lead_need(d, s)

        @pl.when(lead_any)
        def _():
            @pl.loop(0, cell_rows // tile)
            def _(b):
                rows = pl.ds(pl.multiple_of(b * tile, tile), tile)
                h = contract(x_t[rows, :], w_t[...], 1, 0)
                h = jnp.tanh(h)
                d_hid = contract(dbasis[rows, :], t_out[...], 1, 1)
                dpre_t[rows, :] = ((1.0 - h * h) * d_hid).astype(BF16)

        def t_copy(at, d):
            slot = lax.rem(c + cells - d, cells) - 1
            return pltpu.make_async_remote_copy(
                src_ref=t_send.at[at], dst_ref=t_recv.at[slot], send_sem=t_ss.at[at],
                recv_sem=t_rs.at[slot], device_id={"cell": d}, device_id_type=MESH)

        for at, d in reversed(list(enumerate(trunk_dests))):
            @pl.when(trunk_need(d, s))
            def _():
                base = (d * scens + s) * own_rows
                pick = contract(
                    choose(pad_rows, twidth, base, 1, branch_rows + trunk_lead), hid_t[...], 1, 1)
                total[...] = contract(pick.astype(BF16), dbasis[...], 1, 0)

                @pl.when(lead_need(d, s))
                def _():
                    pick = contract(
                        choose(pad_rows, feats + 128, base, 1, branch_rows)
                        * (lax.broadcasted_iota(jnp.int32, (pad_rows, feats + 128), 1)
                           < trunk_lead).astype(F32).astype(BF16),
                        x_t[...], 1, 1)
                    total[...] += contract(pick.astype(BF16), dpre_t[...], 1, 0)

                @pl.when(c == d)
                def _():
                    t_own[...] = total[...]

                @pl.when(c != d)
                def _():
                    t_send[at] = total[...].astype(BF16)
                    t_copy(at, d).start()

        for copy in z_copies:
            copy.wait()
        d_copies = [to_scen(dc.at[s], dc.at[s], d_ss, d_rs, k) for k in range(1, scens)]
        for copy in d_copies:
            copy.start()

        has_in = first < in_rows
        has_hid = (first + own_rows > in_rows) & (first < branch_rows)
        has_trunk = first + own_rows > branch_rows
        x_whole = x_all.reshape(all_scen, samples + 128)
        hid_whole = hid.reshape(all_scen, bwidth)

        @pl.when(has_in)
        def _():
            keep = (lax.broadcasted_iota(jnp.int32, (pad_rows, samples + 128), 1)
                    < samples + groups).astype(F32).astype(BF16)
            pick_in0[...] = contract(choose(pad_rows, samples + 128, first, 2, 0) * keep,
                                     x_whole[...], 1, 1).astype(BF16)
            pick_in1[...] = contract(choose(pad_rows, samples + 128, first, 2, 1) * keep,
                                     x_whole[...], 1, 1).astype(BF16)

        @pl.when(has_hid)
        def _():
            pick_hid[...] = contract(choose(pad_rows, bwidth, first, 1, in_rows),
                                     hid_whole[...], 1, 1).astype(BF16)

        total[...] = jnp.zeros_like(total)
        for copy in d_copies:
            copy.wait()
        dc_whole = dc.reshape(all_scen, WIDE)

        @pl.when(has_hid)
        def _():
            total[...] += contract(pick_hid[...], dc_whole[...], 1, 0)

        @pl.when(has_in)
        def _():
            dc_rows = dc.reshape(scens, scen_rows, WIDE)
            @pl.loop(0, scens)
            def _(p):
                d_hid = contract(dc_rows[p], b_out[...], 1, 1)
                rows = pl.ds(pl.multiple_of(p * scen_rows, scen_rows), scen_rows)
                dpre_b[rows, :] = (d_hid * dgelu[p]).astype(BF16)
            total[...] += contract(pick_in0[...], dpre_b[:, :WIDE], 1, 0)
            total[...] += contract(pick_in1[...], dpre_b[:, WIDE:], 1, 0)

        @pl.when(has_trunk)
        def _():
            total[...] += t_own[...]
            for k in range(cells - 1):
                pltpu.make_async_remote_copy(
                    src_ref=t_send.at[0], dst_ref=t_recv.at[k], send_sem=t_ss.at[0],
                    recv_sem=t_rs.at[k], device_id={"cell": cell_at(1)},
                    device_id_type=MESH).wait_recv()
                total[...] += t_recv[k].astype(F32)

        for j in range(WIDE // 128):
            out[pl.ds(j, own_rows, WIDE // 128), :] = total[0:own_rows, j * 128:(j + 1) * 128]

        for at, d in enumerate(trunk_dests):
            @pl.when(trunk_need(d, s) & (c != d))
            def _():
                t_copy(at, d).wait_send()

    dma = pltpu.SemaphoreType.DMA
    scratch = [
        pltpu.VMEM((scens, scen_rows, samples + 128), BF16),
        pltpu.VMEM((samples + 128, bwidth), BF16),
        pltpu.VMEM((feats + 128, twidth), BF16),
        pltpu.VMEM((cell_rows, feats + 128), BF16),
        pltpu.VMEM((scens, scen_rows, bwidth), F32),
        pltpu.VMEM((scens, scen_rows, bwidth), BF16),
        pltpu.VMEM((scens, scen_rows, WIDE), BF16),
        pltpu.VMEM((cell_rows, twidth), BF16),
        pltpu.VMEM((cell_rows, WIDE), BF16),
        pltpu.VMEM((scens, scen_rows, cell_rows), BF16),
        pltpu.VMEM((cells, chunk, WIDE), F32),
        pltpu.VMEM((cells, chunk, WIDE), BF16),
        pltpu.VMEM((cells - 1, chunk, WIDE), BF16),
        pltpu.VMEM((scens, cells, chunk, WIDE), BF16),
        pltpu.VMEM((cell_rows, WIDE), BF16),
        pltpu.VMEM((cell_rows, twidth), BF16),
        pltpu.VMEM((pad_rows, all_scen), BF16),
        pltpu.VMEM((pad_rows, all_scen), BF16),
        pltpu.VMEM((pad_rows, all_scen), BF16),
        pltpu.VMEM((pad_rows, WIDE), F32),
        pltpu.VMEM((len(trunk_dests), pad_rows, WIDE), BF16),
        pltpu.VMEM((cells - 1, pad_rows, WIDE), BF16),
        pltpu.VMEM((all_scen, bwidth), BF16),
        pltpu.VMEM((pad_rows, WIDE), F32),
        dma((scens - 1,)), dma((scens - 1,)),
        dma((scens - 1,)), dma((scens - 1,)),
        dma((cells - 1,)), dma((cells - 1,)),
        dma((cells - 1,)), dma((cells - 1,)),
        dma((scens - 1,)), dma((scens - 1,)),
        dma((len(trunk_dests),)), dma((cells - 1,)),
    ]
    return kernel, scratch


def shards(hydrograph, scen_group, cell_feat, cell_class, branch_in, group_table, branch_out,
           trunk_in, class_table, trunk_out, targets):
    cells = lax.axis_size("cell")
    scens = lax.axis_size("scen")
    scen_rows, samples = hydrograph.shape
    cell_rows, feats = cell_feat.shape
    bwidth, width = branch_out.shape
    twidth = trunk_in.shape[1]
    groups, classes = group_table.shape[0], class_table.shape[0]
    size = (samples + groups + width) * bwidth + (feats + classes + width) * twidth
    block = size // (cells * scens)
    fits = (
        cells > 1 and scens > 1 and width == WIDE and twidth == WIDE and bwidth == 2 * WIDE
        and block % WIDE == 0 and block * cells * scens == size
        and scen_rows == 128 and scen_rows % (16 * cells) == 0 and cell_rows % 128 == 0
        and samples == 128 and feats == 128 and groups <= 128 and classes <= 128
        and groups % 16 == 0 and classes % 16 == 0 and scens * scen_rows <= 1024
        and cell_rows <= 512
    )
    if not fits:
        return plain_shards(hydrograph, scen_group, cell_feat, cell_class, branch_in, group_table,
                            branch_out, trunk_in, class_table, trunk_out, targets)
    pairs = float(scen_rows * scens) * float(cell_rows * cells)
    kernel, scratch = make_kernel(cells, scens, scen_rows, cell_rows, bwidth, twidth, groups,
                                  classes, samples, feats, block // WIDE, pairs)
    vmem = pl.BlockSpec(memory_space=pltpu.VMEM)
    smem = pl.BlockSpec(memory_space=pltpu.SMEM)
    out = pl.pallas_call(
        kernel,
        out_shape=jax.ShapeDtypeStruct((block // 128, 128), F32),
        in_specs=[vmem, vmem, vmem, smem] + [vmem] * 7,
        out_specs=vmem,
        scratch_shapes=scratch,
        compiler_params=pltpu.CompilerParams(
            collective_id=0, has_side_effects=True, vmem_limit_bytes=40 * 1024 * 1024),
    )(hydrograph, scen_group.reshape(1, scen_rows), cell_feat, cell_class, branch_in, group_table,
      branch_out, trunk_in, class_table, trunk_out, targets)
    return out.reshape(block)


def solution(mesh):
    in_specs = (
        P(("rep", "scen"), None),
        P(("rep", "scen")),
        P(("rep", "cell"), None),
        P(("rep", "cell")),
        P(),
        P(),
        P(),
        P(),
        P(),
        P(),
        P(("rep", "scen"), "cell"),
    )
    out_specs = P(("rep", "cell", "scen"))
    return jax.shard_map(shards, mesh=mesh, in_specs=in_specs, out_specs=out_specs, check_vma=False)
```

```python
import math

import jax
import jax.numpy as jnp
from jax import lax
from jax.experimental import pallas as pl
from jax.experimental.pallas import tpu as pltpu
from jax.sharding import PartitionSpec as P

MESH = pl.DeviceIdType.MESH
BF16 = jnp.bfloat16
F32 = jnp.float32
WIDE = 512


def contract(left, right, left_dim, right_dim):
    return lax.dot_general(
        left, right, (((left_dim,), (right_dim,)), ((), ())), preferred_element_type=jnp.float32
    )


def plain_shards(
    hydrograph,
    scen_group,
    cell_feat,
    cell_class,
    branch_in,
    group_table,
    branch_out,
    trunk_in,
    class_table,
    trunk_out,
    targets,
):
    cell_count = lax.axis_size("cell")
    scen_count = lax.axis_size("scen")
    whole_pairs = jnp.float32(hydrograph.shape[0] * scen_count) * jnp.float32(
        cell_feat.shape[0] * cell_count
    )
    group_hot = (
        scen_group[:, None] == jnp.arange(group_table.shape[0], dtype=jnp.int32)[None, :]
    ).astype(BF16)
    class_cells = jnp.repeat(cell_class, 128)
    class_hot = (
        class_cells[:, None] == jnp.arange(class_table.shape[0], dtype=jnp.int32)[None, :]
    ).astype(BF16)
    pre_branch = contract(hydrograph, branch_in, 1, 0) + contract(group_hot, group_table, 1, 0)
    hid_branch = jax.nn.gelu(pre_branch).astype(BF16)
    coeff_local = contract(hid_branch, branch_out, 1, 0).astype(BF16)
    pre_trunk = contract(cell_feat, trunk_in, 1, 0) + contract(class_hot, class_table, 1, 0)
    hid_trunk = jnp.tanh(pre_trunk).astype(BF16)
    basis_local = contract(hid_trunk, trunk_out, 1, 0).astype(BF16)
    predicted = contract(coeff_local, basis_local, 1, 1) * (
        1.0 / jnp.sqrt(jnp.float32(branch_out.shape[1]))
    )
    resid = ((predicted - targets) * (1.0 / jnp.sqrt(whole_pairs))).astype(BF16)
    d_coeff = lax.psum(contract(resid, basis_local, 1, 0), "cell").astype(BF16)
    d_basis = lax.psum(contract(resid, coeff_local, 0, 0).astype(BF16), "scen")
    g_branch_out = contract(hid_branch, d_coeff, 0, 0)
    d_hid_branch = contract(d_coeff, branch_out, 1, 1)
    d_pre_branch = jax.vjp(jax.nn.gelu, pre_branch)[1](d_hid_branch)[0].astype(BF16)
    g_branch_in = contract(hydrograph, d_pre_branch, 0, 0)
    g_group_table = contract(group_hot, d_pre_branch, 0, 0)
    g_trunk_out = contract(hid_trunk, d_basis, 0, 0)
    d_hid_trunk = contract(d_basis, trunk_out, 1, 1)
    d_pre_trunk = jax.vjp(jnp.tanh, pre_trunk)[1](d_hid_trunk)[0].astype(BF16)
    g_trunk_in = contract(cell_feat, d_pre_trunk, 0, 0)
    g_class_table = contract(class_hot, d_pre_trunk, 0, 0)
    branch_flat = jnp.concatenate(
        [g_branch_in.ravel(), g_group_table.ravel(), g_branch_out.ravel()]
    )
    trunk_flat = jnp.concatenate([g_trunk_in.ravel(), g_class_table.ravel(), g_trunk_out.ravel()])
    branch_flat = branch_flat * (lax.axis_index("cell") == 0).astype(F32)
    trunk_flat = trunk_flat * (lax.axis_index("scen") == 0).astype(F32)
    flat_grad = jnp.concatenate([branch_flat, trunk_flat])
    return lax.psum_scatter(flat_grad, ("cell", "scen"), scatter_dimension=0, tiled=True)


def choose(rows, cols, first, scale, offset):
    row = lax.broadcasted_iota(jnp.int32, (rows, cols), 0) + first
    col = lax.broadcasted_iota(jnp.int32, (rows, cols), 1) * scale + offset
    return (row == col).astype(F32).astype(BF16)


def make_kernel(cells, scens, scen_rows, cell_rows, bwidth, twidth, groups, classes, samples, feats,
                own_rows, pairs):
    pad_rows = -(-own_rows // 16) * 16
    chunk = scen_rows // cells
    in_rows = 2 * (samples + groups)
    branch_rows = in_rows + bwidth
    trunk_lead = feats + classes
    all_scen = scens * scen_rows
    inv_root = 1.0 / math.sqrt(WIDE)
    inv_pairs = 1.0 / math.sqrt(pairs)
    trunk_dests = [
        d for d in range(cells) if ((d + 1) * scens) * own_rows > branch_rows
    ]
    tile = 128

    def kernel(hydro, group_h, feat, klass_h, b_in, g_tab, b_out_h, t_in, c_tab, t_out_h,
               targets_h, out,
               group, klass, b_out, t_out, targets, in_sem, x_all, w_b, w_t, x_t, dgelu, hid, coeff, hid_t, basis, resid, part_f, part_b,
               part_in, dc, dbasis, dpre_t, pick_in0, pick_in1, pick_hid, t_own, t_send, t_recv,
               dpre_b, total,
               x_ss, x_rs, r_ss, r_rs, p_ss, p_rs, z_ss, z_rs, d_ss, d_rs, t_ss, t_rs):
        c = lax.axis_index("cell")
        s = lax.axis_index("scen")
        first = (c * scens + s) * own_rows

        def scen_at(k):
            return lax.rem(s + k, scens)

        def cell_at(k):
            return lax.rem(c + k, cells)

        def to_scen(src, dst, ss, rs, k):
            return pltpu.make_async_remote_copy(
                src_ref=src, dst_ref=dst, send_sem=ss.at[k - 1], recv_sem=rs.at[k - 1],
                device_id={"scen": scen_at(k)}, device_id_type=MESH)

        def to_cell(src, dst, ss, rs, k):
            return pltpu.make_async_remote_copy(
                src_ref=src, dst_ref=dst, send_sem=ss.at[k - 1], recv_sem=rs.at[k - 1],
                device_id={"cell": cell_at(k)}, device_id_type=MESH)

        loads = [
            pltpu.make_async_copy(src, dst, in_sem.at[at])
            for at, (src, dst) in enumerate([
                (group_h, group),
                (hydro, x_all.at[s, :, 0:samples]),
                (b_in, w_b.at[0:samples]),
                (g_tab, w_b.at[samples:samples + groups]),
                (b_out_h, b_out),
                (feat, x_t.at[:, 0:feats]),
                (klass_h, klass),
                (t_in, w_t.at[0:feats]),
                (c_tab, w_t.at[feats:feats + classes]),
                (t_out_h, t_out),
                (targets_h, targets),
            ])
        ]
        for load in loads:
            load.start()
        barrier = pltpu.get_barrier_semaphore()
        for k in range(1, scens):
            pl.semaphore_signal(barrier, inc=1, device_id={"scen": scen_at(k)}, device_id_type=MESH)
        for k in range(1, cells):
            pl.semaphore_signal(barrier, inc=1, device_id={"cell": cell_at(k)}, device_id_type=MESH)

        loads[0].wait()
        loads[1].wait()
        hot = (lax.broadcasted_iota(jnp.int32, (128, scen_rows), 0) == group[...]).astype(F32)
        x_all[s, :, samples:samples + 128] = hot.T.astype(BF16)
        pl.semaphore_wait(barrier, scens + cells - 2)
        x_copies = [to_scen(x_all.at[s], x_all.at[s], x_ss, x_rs, k) for k in range(1, scens)]
        for copy in x_copies:
            copy.start()

        w_b[samples + groups:, :] = jnp.zeros((128 - groups, bwidth), BF16)
        w_t[feats + classes:, :] = jnp.zeros((128 - classes, twidth), BF16)

        def branch(p):
            pre = contract(x_all[p], w_b[...], 1, 0)
            inner = math.sqrt(2.0 / math.pi)
            bent = jnp.tanh(inner * (pre + 0.044715 * (pre * pre * pre)))
            cdf = 0.5 * (1.0 + bent)
            hid[p] = (pre * cdf).astype(BF16)
            dgelu[p] = cdf + (0.5 * inner) * pre * (1.0 - bent * bent) * (
                1.0 + (3.0 * 0.044715) * (pre * pre))
            coeff[p] = contract(hid[p], b_out[...], 1, 0).astype(BF16)

        for load in loads[2:5]:
            load.wait()
        branch(s)
        for load in loads[5:10]:
            load.wait()

        @pl.loop(0, cell_rows // tile)
        def _(b):
            rows = pl.ds(pl.multiple_of(b * tile, tile), tile)
            lane = lax.broadcasted_iota(jnp.int32, (tile, 128), 1)
            x_t[rows, feats:feats + 128] = (lane == klass[b]).astype(F32).astype(BF16)
            pre = contract(x_t[rows, :], w_t[...], 1, 0)
            hid_t[rows, :] = jnp.tanh(pre).astype(BF16)
            basis[rows, :] = contract(hid_t[rows, :], t_out[...], 1, 0).astype(BF16)

        loads[10].wait()
        predicted = contract(coeff[s], basis[...], 1, 1) * inv_root
        resid[s] = ((predicted - targets[...]) * inv_pairs).astype(BF16)
        r_copies = [to_scen(resid.at[s], resid.at[s], r_ss, r_rs, k) for k in range(1, scens)]
        for copy in r_copies:
            copy.start()
        partial = contract(resid[s], basis[...], 1, 0)
        for d in range(cells):
            part_f[d] = partial[d * chunk:(d + 1) * chunk]
            part_b[d] = partial[d * chunk:(d + 1) * chunk].astype(BF16)
        p_copies = [to_cell(part_b.at[cell_at(k)], part_in.at[k - 1], p_ss, p_rs, k)
                    for k in range(1, cells)]
        for copy in p_copies:
            copy.start()

        for copy in x_copies:
            copy.wait()
        @pl.loop(1, scens)
        def _(k):
            branch(lax.rem(s + k, scens))

        for copy in p_copies:
            copy.wait()
        summed = part_f[c]
        for k in range(cells - 1):
            summed = summed + part_in[k].astype(F32)
        dc[s, c] = summed.astype(BF16)
        z_copies = [to_cell(dc.at[s, c], dc.at[s, c], z_ss, z_rs, k) for k in range(1, cells)]
        for copy in z_copies:
            copy.start()

        for copy in r_copies:
            copy.wait()
        @pl.loop(0, cell_rows // tile)
        def _(b):
            cols = pl.ds(pl.multiple_of(b * tile, tile), tile)
            sums = jnp.zeros((tile, WIDE), F32)
            for p in range(scens):
                sums = sums + contract(resid[p, :, cols], coeff[p], 0, 0)
            dbasis[cols, :] = sums.astype(BF16)

        def trunk_need(d, me):
            return (d * scens + me + 1) * own_rows > branch_rows

        def lead_need(d, me):
            return ((d * scens + me + 1) * own_rows > branch_rows) & (
                (d * scens + me) * own_rows < branch_rows + trunk_lead)

        lead_any = lead_need(trunk_dests[0], s)
        for d in trunk_dests[1:]:
            lead_any = lead_any | lead_need(d, s)

        @pl.when(lead_any)
        def _():
            @pl.loop(0, cell_rows // tile)
            def _(b):
                rows = pl.ds(pl.multiple_of(b * tile, tile), tile)
                h = contract(x_t[rows, :], w_t[...], 1, 0)
                h = jnp.tanh(h)
                d_hid = contract(dbasis[rows, :], t_out[...], 1, 1)
                dpre_t[rows, :] = ((1.0 - h * h) * d_hid).astype(BF16)

        def t_copy(at, d):
            slot = lax.rem(c + cells - d, cells) - 1
            return pltpu.make_async_remote_copy(
                src_ref=t_send.at[at], dst_ref=t_recv.at[slot], send_sem=t_ss.at[at],
                recv_sem=t_rs.at[slot], device_id={"cell": d}, device_id_type=MESH)

        for at, d in reversed(list(enumerate(trunk_dests))):
            @pl.when(trunk_need(d, s))
            def _():
                base = (d * scens + s) * own_rows
                pick = contract(
                    choose(pad_rows, twidth, base, 1, branch_rows + trunk_lead), hid_t[...], 1, 1)
                total[...] = contract(pick.astype(BF16), dbasis[...], 1, 0)

                @pl.when(lead_need(d, s))
                def _():
                    pick = contract(
                        choose(pad_rows, feats + 128, base, 1, branch_rows)
                        * (lax.broadcasted_iota(jnp.int32, (pad_rows, feats + 128), 1)
                           < trunk_lead).astype(F32).astype(BF16),
                        x_t[...], 1, 1)
                    total[...] += contract(pick.astype(BF16), dpre_t[...], 1, 0)

                @pl.when(c == d)
                def _():
                    t_own[...] = total[...]

                @pl.when(c != d)
                def _():
                    t_send[at] = total[...].astype(BF16)
                    t_copy(at, d).start()

        for copy in z_copies:
            copy.wait()
        d_copies = [to_scen(dc.at[s], dc.at[s], d_ss, d_rs, k) for k in range(1, scens)]
        for copy in d_copies:
            copy.start()

        has_in = first < in_rows
        has_hid = (first + own_rows > in_rows) & (first < branch_rows)
        has_trunk = first + own_rows > branch_rows
        x_whole = x_all.reshape(all_scen, samples + 128)
        hid_whole = hid.reshape(all_scen, bwidth)

        @pl.when(has_in)
        def _():
            keep = (lax.broadcasted_iota(jnp.int32, (pad_rows, samples + 128), 1)
                    < samples + groups).astype(F32).astype(BF16)
            pick_in0[...] = contract(choose(pad_rows, samples + 128, first, 2, 0) * keep,
                                     x_whole[...], 1, 1).astype(BF16)
            pick_in1[...] = contract(choose(pad_rows, samples + 128, first, 2, 1) * keep,
                                     x_whole[...], 1, 1).astype(BF16)

        @pl.when(has_hid)
        def _():
            pick_hid[...] = contract(choose(pad_rows, bwidth, first, 1, in_rows),
                                     hid_whole[...], 1, 1).astype(BF16)

        total[...] = jnp.zeros_like(total)
        for copy in d_copies:
            copy.wait()
        dc_whole = dc.reshape(all_scen, WIDE)

        @pl.when(has_hid)
        def _():
            total[...] += contract(pick_hid[...], dc_whole[...], 1, 0)

        @pl.when(has_in)
        def _():
            dc_rows = dc.reshape(scens, scen_rows, WIDE)
            @pl.loop(0, scens)
            def _(p):
                d_hid = contract(dc_rows[p], b_out[...], 1, 1)
                rows = pl.ds(pl.multiple_of(p * scen_rows, scen_rows), scen_rows)
                dpre_b[rows, :] = (d_hid * dgelu[p]).astype(BF16)
            total[...] += contract(pick_in0[...], dpre_b[:, :WIDE], 1, 0)
            total[...] += contract(pick_in1[...], dpre_b[:, WIDE:], 1, 0)

        @pl.when(has_trunk)
        def _():
            total[...] += t_own[...]
            for k in range(cells - 1):
                pltpu.make_async_remote_copy(
                    src_ref=t_send.at[0], dst_ref=t_recv.at[k], send_sem=t_ss.at[0],
                    recv_sem=t_rs.at[k], device_id={"cell": cell_at(1)},
                    device_id_type=MESH).wait_recv()
                total[...] += t_recv[k].astype(F32)

        for j in range(WIDE // 128):
            out[pl.ds(j, own_rows, WIDE // 128), :] = total[0:own_rows, j * 128:(j + 1) * 128]

        for at, d in enumerate(trunk_dests):
            @pl.when(trunk_need(d, s) & (c != d))
            def _():
                t_copy(at, d).wait_send()

    dma = pltpu.SemaphoreType.DMA
    scratch = [
        pltpu.VMEM((1, scen_rows), jnp.int32),
        pltpu.SMEM((cell_rows // 128,), jnp.int32),
        pltpu.VMEM((bwidth, WIDE), BF16),
        pltpu.VMEM((twidth, WIDE), BF16),
        pltpu.VMEM((scen_rows, cell_rows), F32),
        dma((11,)),
        pltpu.VMEM((scens, scen_rows, samples + 128), BF16),
        pltpu.VMEM((samples + 128, bwidth), BF16),
        pltpu.VMEM((feats + 128, twidth), BF16),
        pltpu.VMEM((cell_rows, feats + 128), BF16),
        pltpu.VMEM((scens, scen_rows, bwidth), F32),
        pltpu.VMEM((scens, scen_rows, bwidth), BF16),
        pltpu.VMEM((scens, scen_rows, WIDE), BF16),
        pltpu.VMEM((cell_rows, twidth), BF16),
        pltpu.VMEM((cell_rows, WIDE), BF16),
        pltpu.VMEM((scens, scen_rows, cell_rows), BF16),
        pltpu.VMEM((cells, chunk, WIDE), F32),
        pltpu.VMEM((cells, chunk, WIDE), BF16),
        pltpu.VMEM((cells - 1, chunk, WIDE), BF16),
        pltpu.VMEM((scens, cells, chunk, WIDE), BF16),
        pltpu.VMEM((cell_rows, WIDE), BF16),
        pltpu.VMEM((cell_rows, twidth), BF16),
        pltpu.VMEM((pad_rows, all_scen), BF16),
        pltpu.VMEM((pad_rows, all_scen), BF16),
        pltpu.VMEM((pad_rows, all_scen), BF16),
        pltpu.VMEM((pad_rows, WIDE), F32),
        pltpu.VMEM((len(trunk_dests), pad_rows, WIDE), BF16),
        pltpu.VMEM((cells - 1, pad_rows, WIDE), BF16),
        pltpu.VMEM((all_scen, bwidth), BF16),
        pltpu.VMEM((pad_rows, WIDE), F32),
        dma((scens - 1,)), dma((scens - 1,)),
        dma((scens - 1,)), dma((scens - 1,)),
        dma((cells - 1,)), dma((cells - 1,)),
        dma((cells - 1,)), dma((cells - 1,)),
        dma((scens - 1,)), dma((scens - 1,)),
        dma((len(trunk_dests),)), dma((cells - 1,)),
    ]
    return kernel, scratch


def shards(hydrograph, scen_group, cell_feat, cell_class, branch_in, group_table, branch_out,
           trunk_in, class_table, trunk_out, targets):
    cells = lax.axis_size("cell")
    scens = lax.axis_size("scen")
    scen_rows, samples = hydrograph.shape
    cell_rows, feats = cell_feat.shape
    bwidth, width = branch_out.shape
    twidth = trunk_in.shape[1]
    groups, classes = group_table.shape[0], class_table.shape[0]
    size = (samples + groups + width) * bwidth + (feats + classes + width) * twidth
    block = size // (cells * scens)
    fits = (
        cells > 1 and scens > 1 and width == WIDE and twidth == WIDE and bwidth == 2 * WIDE
        and block % WIDE == 0 and block * cells * scens == size
        and scen_rows == 128 and scen_rows % (16 * cells) == 0 and cell_rows % 128 == 0
        and samples == 128 and feats == 128 and groups <= 128 and classes <= 128
        and groups % 16 == 0 and classes % 16 == 0 and scens * scen_rows <= 1024
        and cell_rows <= 512
    )
    if not fits:
        return plain_shards(hydrograph, scen_group, cell_feat, cell_class, branch_in, group_table,
                            branch_out, trunk_in, class_table, trunk_out, targets)
    pairs = float(scen_rows * scens) * float(cell_rows * cells)
    kernel, scratch = make_kernel(cells, scens, scen_rows, cell_rows, bwidth, twidth, groups,
                                  classes, samples, feats, block // WIDE, pairs)
    vmem = pl.BlockSpec(memory_space=pltpu.VMEM)
    hbm = pl.BlockSpec(memory_space=pltpu.HBM)
    out = pl.pallas_call(
        kernel,
        out_shape=jax.ShapeDtypeStruct((block // 128, 128), F32),
        in_specs=[hbm] * 11,
        out_specs=vmem,
        scratch_shapes=scratch,
        compiler_params=pltpu.CompilerParams(
            collective_id=0, has_side_effects=True, vmem_limit_bytes=64 * 1024 * 1024),
    )(hydrograph, scen_group.reshape(1, scen_rows), cell_feat, cell_class, branch_in, group_table,
      branch_out, trunk_in, class_table, trunk_out, targets)
    return out.reshape(block)


def solution(mesh):
    in_specs = (
        P(("rep", "scen"), None),
        P(("rep", "scen")),
        P(("rep", "cell"), None),
        P(("rep", "cell")),
        P(),
        P(),
        P(),
        P(),
        P(),
        P(),
        P(("rep", "scen"), "cell"),
    )
    out_specs = P(("rep", "cell", "scen"))
    return jax.shard_map(shards, mesh=mesh, in_specs=in_specs, out_specs=out_specs, check_vma=False)
```

```python
import math

import jax
import jax.numpy as jnp
from jax import lax
from jax.experimental import pallas as pl
from jax.experimental.pallas import tpu as pltpu
from jax.sharding import PartitionSpec as P

MESH = pl.DeviceIdType.MESH
BF16 = jnp.bfloat16
F32 = jnp.float32
WIDE = 512


def contract(left, right, left_dim, right_dim):
    return lax.dot_general(
        left, right, (((left_dim,), (right_dim,)), ((), ())), preferred_element_type=jnp.float32
    )


def plain_shards(
    hydrograph,
    scen_group,
    cell_feat,
    cell_class,
    branch_in,
    group_table,
    branch_out,
    trunk_in,
    class_table,
    trunk_out,
    targets,
):
    cell_count = lax.axis_size("cell")
    scen_count = lax.axis_size("scen")
    whole_pairs = jnp.float32(hydrograph.shape[0] * scen_count) * jnp.float32(
        cell_feat.shape[0] * cell_count
    )
    group_hot = (
        scen_group[:, None] == jnp.arange(group_table.shape[0], dtype=jnp.int32)[None, :]
    ).astype(BF16)
    class_cells = jnp.repeat(cell_class, 128)
    class_hot = (
        class_cells[:, None] == jnp.arange(class_table.shape[0], dtype=jnp.int32)[None, :]
    ).astype(BF16)
    pre_branch = contract(hydrograph, branch_in, 1, 0) + contract(group_hot, group_table, 1, 0)
    hid_branch = jax.nn.gelu(pre_branch).astype(BF16)
    coeff_local = contract(hid_branch, branch_out, 1, 0).astype(BF16)
    pre_trunk = contract(cell_feat, trunk_in, 1, 0) + contract(class_hot, class_table, 1, 0)
    hid_trunk = jnp.tanh(pre_trunk).astype(BF16)
    basis_local = contract(hid_trunk, trunk_out, 1, 0).astype(BF16)
    predicted = contract(coeff_local, basis_local, 1, 1) * (
        1.0 / jnp.sqrt(jnp.float32(branch_out.shape[1]))
    )
    resid = ((predicted - targets) * (1.0 / jnp.sqrt(whole_pairs))).astype(BF16)
    d_coeff = lax.psum(contract(resid, basis_local, 1, 0), "cell").astype(BF16)
    d_basis = lax.psum(contract(resid, coeff_local, 0, 0).astype(BF16), "scen")
    g_branch_out = contract(hid_branch, d_coeff, 0, 0)
    d_hid_branch = contract(d_coeff, branch_out, 1, 1)
    d_pre_branch = jax.vjp(jax.nn.gelu, pre_branch)[1](d_hid_branch)[0].astype(BF16)
    g_branch_in = contract(hydrograph, d_pre_branch, 0, 0)
    g_group_table = contract(group_hot, d_pre_branch, 0, 0)
    g_trunk_out = contract(hid_trunk, d_basis, 0, 0)
    d_hid_trunk = contract(d_basis, trunk_out, 1, 1)
    d_pre_trunk = jax.vjp(jnp.tanh, pre_trunk)[1](d_hid_trunk)[0].astype(BF16)
    g_trunk_in = contract(cell_feat, d_pre_trunk, 0, 0)
    g_class_table = contract(class_hot, d_pre_trunk, 0, 0)
    branch_flat = jnp.concatenate(
        [g_branch_in.ravel(), g_group_table.ravel(), g_branch_out.ravel()]
    )
    trunk_flat = jnp.concatenate([g_trunk_in.ravel(), g_class_table.ravel(), g_trunk_out.ravel()])
    branch_flat = branch_flat * (lax.axis_index("cell") == 0).astype(F32)
    trunk_flat = trunk_flat * (lax.axis_index("scen") == 0).astype(F32)
    flat_grad = jnp.concatenate([branch_flat, trunk_flat])
    return lax.psum_scatter(flat_grad, ("cell", "scen"), scatter_dimension=0, tiled=True)


def choose(rows, cols, first, scale, offset):
    row = lax.broadcasted_iota(jnp.int32, (rows, cols), 0) + first
    col = lax.broadcasted_iota(jnp.int32, (rows, cols), 1) * scale + offset
    return (row == col).astype(F32).astype(BF16)


def make_kernel(cells, scens, scen_rows, cell_rows, bwidth, twidth, groups, classes, samples, feats,
                own_rows, pairs):
    pad_rows = -(-own_rows // 16) * 16
    chunk = scen_rows // cells
    in_rows = 2 * (samples + groups)
    branch_rows = in_rows + bwidth
    trunk_lead = feats + classes
    all_scen = scens * scen_rows
    inv_root = 1.0 / math.sqrt(WIDE)
    inv_pairs = 1.0 / math.sqrt(pairs)
    trunk_dests = [
        d for d in range(cells) if ((d + 1) * scens) * own_rows > branch_rows
    ]
    tile = 128
    branch_cells = -(-branch_rows // (scens * own_rows))

    def kernel(hydro, group_h, feat, klass_h, b_in, g_tab, b_out_h, t_in, c_tab, t_out_h,
               targets_h, out,
               group, klass, b_out, t_out, targets, in_sem, x_all, w_b, w_t, x_t, dgelu, hid, coeff, hid_t, basis, resid, part_f, part_b,
               part_in, dc, dbasis, dpre_t, pick_in0, pick_in1, pick_hid, t_own, t_send, t_recv, t_mid, t_relay,
               dpre_b, total,
               x_ss, x_rs, r_ss, r_rs, p_ss, p_rs, z_ss, z_rs, f_ss, f_rs, n_ss, n_rs, g_ss, g_rs, t_ss, t_rs, m_rs):
        c = lax.axis_index("cell")
        s = lax.axis_index("scen")
        first = (c * scens + s) * own_rows

        def scen_at(k):
            return lax.rem(s + k, scens)

        def cell_at(k):
            return lax.rem(c + k, cells)

        sibling = s + 1 - 2 * lax.rem(s, 2)
        far = lax.rem(s + scens // 2, scens)

        def to_peer(ref, ss, rs, at, peer):
            return pltpu.make_async_remote_copy(
                src_ref=ref, dst_ref=ref, send_sem=ss.at[at], recv_sem=rs.at[at],
                device_id={"scen": peer}, device_id_type=MESH)

        def to_scen(src, dst, ss, rs, k):
            return pltpu.make_async_remote_copy(
                src_ref=src, dst_ref=dst, send_sem=ss.at[k - 1], recv_sem=rs.at[k - 1],
                device_id={"scen": scen_at(k)}, device_id_type=MESH)

        def to_cell(src, dst, ss, rs, k):
            return pltpu.make_async_remote_copy(
                src_ref=src, dst_ref=dst, send_sem=ss.at[k - 1], recv_sem=rs.at[k - 1],
                device_id={"cell": cell_at(k)}, device_id_type=MESH)

        loads = [
            pltpu.make_async_copy(src, dst, in_sem.at[at])
            for at, (src, dst) in enumerate([
                (group_h, group),
                (hydro, x_all.at[s, :, 0:samples]),
                (b_in, w_b.at[0:samples]),
                (g_tab, w_b.at[samples:samples + groups]),
                (b_out_h, b_out),
                (feat, x_t.at[:, 0:feats]),
                (klass_h, klass),
                (t_in, w_t.at[0:feats]),
                (c_tab, w_t.at[feats:feats + classes]),
                (t_out_h, t_out),
                (targets_h, targets),
            ])
        ]
        for load in loads:
            load.start()
        barrier = pltpu.get_barrier_semaphore()
        for k in range(1, scens):
            pl.semaphore_signal(barrier, inc=1, device_id={"scen": scen_at(k)}, device_id_type=MESH)
        for k in range(1, cells):
            pl.semaphore_signal(barrier, inc=1, device_id={"cell": cell_at(k)}, device_id_type=MESH)

        loads[0].wait()
        loads[1].wait()
        hot = (lax.broadcasted_iota(jnp.int32, (128, scen_rows), 0) == group[...]).astype(F32)
        x_all[s, :, samples:samples + 128] = hot.T.astype(BF16)
        pl.semaphore_wait(barrier, scens + cells - 2)
        x_copies = [to_scen(x_all.at[s], x_all.at[s], x_ss, x_rs, k) for k in range(1, scens)]
        for copy in x_copies:
            copy.start()

        w_b[samples + groups:, :] = jnp.zeros((128 - groups, bwidth), BF16)
        w_t[feats + classes:, :] = jnp.zeros((128 - classes, twidth), BF16)

        def branch(p):
            pre = contract(x_all[p], w_b[...], 1, 0)
            inner = math.sqrt(2.0 / math.pi)
            bent = jnp.tanh(inner * (pre + 0.044715 * (pre * pre * pre)))
            cdf = 0.5 * (1.0 + bent)
            hid[p] = (pre * cdf).astype(BF16)
            dgelu[p] = cdf + (0.5 * inner) * pre * (1.0 - bent * bent) * (
                1.0 + (3.0 * 0.044715) * (pre * pre))
            coeff[p] = contract(hid[p], b_out[...], 1, 0).astype(BF16)

        for load in loads[2:5]:
            load.wait()
        branch(s)
        for load in loads[5:10]:
            load.wait()

        @pl.loop(0, cell_rows // tile)
        def _(b):
            rows = pl.ds(pl.multiple_of(b * tile, tile), tile)
            lane = lax.broadcasted_iota(jnp.int32, (tile, 128), 1)
            x_t[rows, feats:feats + 128] = (lane == klass[b]).astype(F32).astype(BF16)
            pre = contract(x_t[rows, :], w_t[...], 1, 0)
            hid_t[rows, :] = jnp.tanh(pre).astype(BF16)
            basis[rows, :] = contract(hid_t[rows, :], t_out[...], 1, 0).astype(BF16)

        loads[10].wait()
        predicted = contract(coeff[s], basis[...], 1, 1) * inv_root
        resid[s] = ((predicted - targets[...]) * inv_pairs).astype(BF16)
        r_far = to_peer(resid.at[s], r_ss, r_rs, 0, far)
        r_far.start()
        r_near = to_peer(resid.at[s], r_ss, r_rs, 1, sibling)
        r_near.start()
        partial = contract(resid[s], basis[...], 1, 0)
        for d in range(cells):
            part_f[d] = partial[d * chunk:(d + 1) * chunk]
            part_b[d] = partial[d * chunk:(d + 1) * chunk].astype(BF16)
        p_copies = [to_cell(part_b.at[cell_at(k)], part_in.at[k - 1], p_ss, p_rs, k)
                    for k in range(1, cells)]
        for copy in p_copies:
            copy.start()

        for copy in x_copies:
            copy.wait()
        @pl.loop(1, scens)
        def _(k):
            branch(lax.rem(s + k, scens))

        r_far.wait()
        r_pass = to_peer(resid.at[far], r_ss, r_rs, 2, sibling)
        r_pass.start()
        for copy in p_copies:
            copy.wait()
        summed = part_f[c]
        for k in range(cells - 1):
            summed = summed + part_in[k].astype(F32)
        dc[s, c] = summed.astype(BF16)
        z_copies = [to_cell(dc.at[s, c], dc.at[s, c], z_ss, z_rs, k) for k in range(1, cells)]
        takes_dc = c < branch_cells

        def share(j):
            chunk_at = dc.at[s, lax.rem(c + cells - j, cells)]
            return [to_peer(chunk_at, f_ss, f_rs, j, far), to_peer(chunk_at, n_ss, n_rs, j, sibling)]

        def pass_on(j):
            return to_peer(dc.at[far, lax.rem(c + cells - j, cells)], g_ss, g_rs, j, sibling)

        for k, copy in enumerate(z_copies):
            @pl.when(cell_at(k + 1) < branch_cells)
            def _():
                copy.start()

        @pl.when(takes_dc)
        def _():
            for copy in share(0):
                copy.start()

        r_near.wait()
        r_pass.wait()
        @pl.loop(0, cell_rows // tile)
        def _(b):
            cols = pl.ds(pl.multiple_of(b * tile, tile), tile)
            sums = jnp.zeros((tile, WIDE), F32)
            for p in range(scens):
                sums = sums + contract(resid[p, :, cols], coeff[p], 0, 0)
            dbasis[cols, :] = sums.astype(BF16)

        def trunk_need(d, me):
            return (d * scens + me + 1) * own_rows > branch_rows

        def lead_need(d, me):
            return ((d * scens + me + 1) * own_rows > branch_rows) & (
                (d * scens + me) * own_rows < branch_rows + trunk_lead)

        lead_any = lead_need(trunk_dests[0], s)
        for d in trunk_dests[1:]:
            lead_any = lead_any | lead_need(d, s)

        @pl.when(lead_any)
        def _():
            @pl.loop(0, cell_rows // tile)
            def _(b):
                rows = pl.ds(pl.multiple_of(b * tile, tile), tile)
                h = contract(x_t[rows, :], w_t[...], 1, 0)
                h = jnp.tanh(h)
                d_hid = contract(dbasis[rows, :], t_out[...], 1, 1)
                dpre_t[rows, :] = ((1.0 - h * h) * d_hid).astype(BF16)

        def t_copy(at, d, relay):
            return pltpu.make_async_remote_copy(
                src_ref=t_send.at[at], dst_ref=t_recv.at[relay], send_sem=t_ss.at[at],
                recv_sem=t_rs.at[relay], device_id={"cell": d}, device_id_type=MESH)

        def m_copy(at):
            return pltpu.make_async_remote_copy(
                src_ref=t_send.at[at], dst_ref=t_mid.at[at], send_sem=t_ss.at[at],
                recv_sem=m_rs.at[at], device_id={"cell": 1}, device_id_type=MESH)

        for at, d in reversed(list(enumerate(trunk_dests))):
            @pl.when(trunk_need(d, s))
            def _():
                base = (d * scens + s) * own_rows
                pick = contract(
                    choose(pad_rows, twidth, base, 1, branch_rows + trunk_lead), hid_t[...], 1, 1)
                total[...] = contract(pick.astype(BF16), dbasis[...], 1, 0)

                @pl.when(lead_need(d, s))
                def _():
                    pick = contract(
                        choose(pad_rows, feats + 128, base, 1, branch_rows)
                        * (lax.broadcasted_iota(jnp.int32, (pad_rows, feats + 128), 1)
                           < trunk_lead).astype(F32).astype(BF16),
                        x_t[...], 1, 1)
                    total[...] += contract(pick.astype(BF16), dpre_t[...], 1, 0)

                @pl.when(c == d)
                def _():
                    t_own[...] = total[...]

                @pl.when(c == 1)
                def _():
                    t_relay[at] = total[...]

                @pl.when((c != d) & (c != 1))
                def _():
                    t_send[at] = total[...].astype(BF16)

                @pl.when((c != d) & (c > 1))
                def _():
                    t_copy(at, d, 0).start()

                @pl.when(c == 0)
                def _():
                    m_copy(at).start()

        for k, copy in enumerate(z_copies):
            @pl.when(takes_dc)
            def _():
                copy.wait_recv()
                for other in share(k + 1):
                    other.start()

        for j in range(cells):
            @pl.when(takes_dc)
            def _():
                share(j)[0].wait_recv()
                pass_on(j).start()

        has_in = first < in_rows
        has_hid = (first + own_rows > in_rows) & (first < branch_rows)
        has_trunk = first + own_rows > branch_rows
        x_whole = x_all.reshape(all_scen, samples + 128)
        hid_whole = hid.reshape(all_scen, bwidth)

        @pl.when(has_in)
        def _():
            keep = (lax.broadcasted_iota(jnp.int32, (pad_rows, samples + 128), 1)
                    < samples + groups).astype(F32).astype(BF16)
            pick_in0[...] = contract(choose(pad_rows, samples + 128, first, 2, 0) * keep,
                                     x_whole[...], 1, 1).astype(BF16)
            pick_in1[...] = contract(choose(pad_rows, samples + 128, first, 2, 1) * keep,
                                     x_whole[...], 1, 1).astype(BF16)

        @pl.when(has_hid)
        def _():
            pick_hid[...] = contract(choose(pad_rows, bwidth, first, 1, in_rows),
                                     hid_whole[...], 1, 1).astype(BF16)

        for at, d in reversed(list(enumerate(trunk_dests))):
            @pl.when(trunk_need(d, s) & (c == 1))
            def _():
                m_copy(at).wait_recv()
                t_send[at] = (t_relay[at] + t_mid[at].astype(F32)).astype(BF16)
                t_copy(at, d, 1).start()

        total[...] = jnp.zeros_like(total)
        @pl.when(takes_dc)
        def _():
            for j in range(cells):
                share(j)[1].wait_recv()
                pass_on(j).wait_recv()
        dc_whole = dc.reshape(all_scen, WIDE)

        @pl.when(has_hid)
        def _():
            total[...] += contract(pick_hid[...], dc_whole[...], 1, 0)

        @pl.when(has_in)
        def _():
            dc_rows = dc.reshape(scens, scen_rows, WIDE)
            @pl.loop(0, scens)
            def _(p):
                d_hid = contract(dc_rows[p], b_out[...], 1, 1)
                rows = pl.ds(pl.multiple_of(p * scen_rows, scen_rows), scen_rows)
                dpre_b[rows, :] = (d_hid * dgelu[p]).astype(BF16)
            total[...] += contract(pick_in0[...], dpre_b[:, :WIDE], 1, 0)
            total[...] += contract(pick_in1[...], dpre_b[:, WIDE:], 1, 0)

        @pl.when(has_trunk)
        def _():
            total[...] += t_own[...]
            for k in range(2):
                t_copy(0, 0, k).wait_recv()
                total[...] += t_recv[k].astype(F32)

        for j in range(WIDE // 128):
            out[pl.ds(j, own_rows, WIDE // 128), :] = total[0:own_rows, j * 128:(j + 1) * 128]

        for k, copy in enumerate(z_copies):
            @pl.when(cell_at(k + 1) < branch_cells)
            def _():
                copy.wait_send()

        @pl.when(takes_dc)
        def _():
            for j in range(cells):
                for copy in share(j) + [pass_on(j)]:
                    copy.wait_send()

        for at, d in enumerate(trunk_dests):
            @pl.when(trunk_need(d, s) & (c != d))
            def _():
                t_copy(at, d, 0).wait_send()

    dma = pltpu.SemaphoreType.DMA
    scratch = [
        pltpu.VMEM((1, scen_rows), jnp.int32),
        pltpu.SMEM((cell_rows // 128,), jnp.int32),
        pltpu.VMEM((bwidth, WIDE), BF16),
        pltpu.VMEM((twidth, WIDE), BF16),
        pltpu.VMEM((scen_rows, cell_rows), F32),
        dma((11,)),
        pltpu.VMEM((scens, scen_rows, samples + 128), BF16),
        pltpu.VMEM((samples + 128, bwidth), BF16),
        pltpu.VMEM((feats + 128, twidth), BF16),
        pltpu.VMEM((cell_rows, feats + 128), BF16),
        pltpu.VMEM((scens, scen_rows, bwidth), F32),
        pltpu.VMEM((scens, scen_rows, bwidth), BF16),
        pltpu.VMEM((scens, scen_rows, WIDE), BF16),
        pltpu.VMEM((cell_rows, twidth), BF16),
        pltpu.VMEM((cell_rows, WIDE), BF16),
        pltpu.VMEM((scens, scen_rows, cell_rows), BF16),
        pltpu.VMEM((cells, chunk, WIDE), F32),
        pltpu.VMEM((cells, chunk, WIDE), BF16),
        pltpu.VMEM((cells - 1, chunk, WIDE), BF16),
        pltpu.VMEM((scens, cells, chunk, WIDE), BF16),
        pltpu.VMEM((cell_rows, WIDE), BF16),
        pltpu.VMEM((cell_rows, twidth), BF16),
        pltpu.VMEM((pad_rows, all_scen), BF16),
        pltpu.VMEM((pad_rows, all_scen), BF16),
        pltpu.VMEM((pad_rows, all_scen), BF16),
        pltpu.VMEM((pad_rows, WIDE), F32),
        pltpu.VMEM((len(trunk_dests), pad_rows, WIDE), BF16),
        pltpu.VMEM((2, pad_rows, WIDE), BF16),
        pltpu.VMEM((len(trunk_dests), pad_rows, WIDE), BF16),
        pltpu.VMEM((len(trunk_dests), pad_rows, WIDE), F32),
        pltpu.VMEM((all_scen, bwidth), BF16),
        pltpu.VMEM((pad_rows, WIDE), F32),
        dma((scens - 1,)), dma((scens - 1,)),
        dma((scens - 1,)), dma((scens - 1,)),
        dma((cells - 1,)), dma((cells - 1,)),
        dma((cells - 1,)), dma((cells - 1,)),
        dma((cells,)), dma((cells,)),
        dma((cells,)), dma((cells,)),
        dma((cells,)), dma((cells,)),
        dma((len(trunk_dests),)), dma((2,)), dma((len(trunk_dests),)),
    ]
    return kernel, scratch


def shards(hydrograph, scen_group, cell_feat, cell_class, branch_in, group_table, branch_out,
           trunk_in, class_table, trunk_out, targets):
    cells = lax.axis_size("cell")
    scens = lax.axis_size("scen")
    scen_rows, samples = hydrograph.shape
    cell_rows, feats = cell_feat.shape
    bwidth, width = branch_out.shape
    twidth = trunk_in.shape[1]
    groups, classes = group_table.shape[0], class_table.shape[0]
    size = (samples + groups + width) * bwidth + (feats + classes + width) * twidth
    block = size // (cells * scens)
    fits = (
        cells == 4 and scens == 4 and width == WIDE and twidth == WIDE and bwidth == 2 * WIDE
        and block % WIDE == 0 and block * cells * scens == size
        and scen_rows == 128 and scen_rows % (16 * cells) == 0 and cell_rows % 128 == 0
        and samples == 128 and feats == 128 and groups <= 128 and classes <= 128
        and groups % 16 == 0 and classes % 16 == 0 and scens * scen_rows <= 1024
        and cell_rows <= 512 and (samples + groups) * 2 + bwidth >= 2 * scens * (block // WIDE)
    )
    if not fits:
        return plain_shards(hydrograph, scen_group, cell_feat, cell_class, branch_in, group_table,
                            branch_out, trunk_in, class_table, trunk_out, targets)
    pairs = float(scen_rows * scens) * float(cell_rows * cells)
    kernel, scratch = make_kernel(cells, scens, scen_rows, cell_rows, bwidth, twidth, groups,
                                  classes, samples, feats, block // WIDE, pairs)
    vmem = pl.BlockSpec(memory_space=pltpu.VMEM)
    hbm = pl.BlockSpec(memory_space=pltpu.HBM)
    out = pl.pallas_call(
        kernel,
        out_shape=jax.ShapeDtypeStruct((block // 128, 128), F32),
        in_specs=[hbm] * 11,
        out_specs=vmem,
        scratch_shapes=scratch,
        compiler_params=pltpu.CompilerParams(
            collective_id=0, has_side_effects=True, vmem_limit_bytes=64 * 1024 * 1024),
    )(hydrograph, scen_group.reshape(1, scen_rows), cell_feat, cell_class, branch_in, group_table,
      branch_out, trunk_in, class_table, trunk_out, targets)
    return out.reshape(block)


def solution(mesh):
    in_specs = (
        P(("rep", "scen"), None),
        P(("rep", "scen")),
        P(("rep", "cell"), None),
        P(("rep", "cell")),
        P(),
        P(),
        P(),
        P(),
        P(),
        P(),
        P(("rep", "scen"), "cell"),
    )
    out_specs = P(("rep", "cell", "scen"))
    return jax.shard_map(shards, mesh=mesh, in_specs=in_specs, out_specs=out_specs, check_vma=False)
```

```python
import math

import jax
import jax.numpy as jnp
from jax import lax
from jax.experimental import pallas as pl
from jax.experimental.pallas import tpu as pltpu
from jax.sharding import PartitionSpec as P

MESH = pl.DeviceIdType.MESH
BF16 = jnp.bfloat16
F32 = jnp.float32
WIDE = 512


def contract(left, right, left_dim, right_dim):
    return lax.dot_general(
        left, right, (((left_dim,), (right_dim,)), ((), ())), preferred_element_type=jnp.float32
    )


def plain_shards(
    hydrograph,
    scen_group,
    cell_feat,
    cell_class,
    branch_in,
    group_table,
    branch_out,
    trunk_in,
    class_table,
    trunk_out,
    targets,
):
    cell_count = lax.axis_size("cell")
    scen_count = lax.axis_size("scen")
    whole_pairs = jnp.float32(hydrograph.shape[0] * scen_count) * jnp.float32(
        cell_feat.shape[0] * cell_count
    )
    group_hot = (
        scen_group[:, None] == jnp.arange(group_table.shape[0], dtype=jnp.int32)[None, :]
    ).astype(BF16)
    class_cells = jnp.repeat(cell_class, 128)
    class_hot = (
        class_cells[:, None] == jnp.arange(class_table.shape[0], dtype=jnp.int32)[None, :]
    ).astype(BF16)
    pre_branch = contract(hydrograph, branch_in, 1, 0) + contract(group_hot, group_table, 1, 0)
    hid_branch = jax.nn.gelu(pre_branch).astype(BF16)
    coeff_local = contract(hid_branch, branch_out, 1, 0).astype(BF16)
    pre_trunk = contract(cell_feat, trunk_in, 1, 0) + contract(class_hot, class_table, 1, 0)
    hid_trunk = jnp.tanh(pre_trunk).astype(BF16)
    basis_local = contract(hid_trunk, trunk_out, 1, 0).astype(BF16)
    predicted = contract(coeff_local, basis_local, 1, 1) * (
        1.0 / jnp.sqrt(jnp.float32(branch_out.shape[1]))
    )
    resid = ((predicted - targets) * (1.0 / jnp.sqrt(whole_pairs))).astype(BF16)
    d_coeff = lax.psum(contract(resid, basis_local, 1, 0), "cell").astype(BF16)
    d_basis = lax.psum(contract(resid, coeff_local, 0, 0).astype(BF16), "scen")
    g_branch_out = contract(hid_branch, d_coeff, 0, 0)
    d_hid_branch = contract(d_coeff, branch_out, 1, 1)
    d_pre_branch = jax.vjp(jax.nn.gelu, pre_branch)[1](d_hid_branch)[0].astype(BF16)
    g_branch_in = contract(hydrograph, d_pre_branch, 0, 0)
    g_group_table = contract(group_hot, d_pre_branch, 0, 0)
    g_trunk_out = contract(hid_trunk, d_basis, 0, 0)
    d_hid_trunk = contract(d_basis, trunk_out, 1, 1)
    d_pre_trunk = jax.vjp(jnp.tanh, pre_trunk)[1](d_hid_trunk)[0].astype(BF16)
    g_trunk_in = contract(cell_feat, d_pre_trunk, 0, 0)
    g_class_table = contract(class_hot, d_pre_trunk, 0, 0)
    branch_flat = jnp.concatenate(
        [g_branch_in.ravel(), g_group_table.ravel(), g_branch_out.ravel()]
    )
    trunk_flat = jnp.concatenate([g_trunk_in.ravel(), g_class_table.ravel(), g_trunk_out.ravel()])
    branch_flat = branch_flat * (lax.axis_index("cell") == 0).astype(F32)
    trunk_flat = trunk_flat * (lax.axis_index("scen") == 0).astype(F32)
    flat_grad = jnp.concatenate([branch_flat, trunk_flat])
    return lax.psum_scatter(flat_grad, ("cell", "scen"), scatter_dimension=0, tiled=True)


def choose(rows, cols, first, scale, offset):
    row = lax.broadcasted_iota(jnp.int32, (rows, cols), 0) + first
    col = lax.broadcasted_iota(jnp.int32, (rows, cols), 1) * scale + offset
    return (row == col).astype(F32).astype(BF16)


def make_kernel(cells, scens, scen_rows, cell_rows, bwidth, twidth, groups, classes, samples, feats,
                own_rows, pairs):
    pad_rows = -(-own_rows // 32) * 32
    chunk = scen_rows // cells
    in_rows = 2 * (samples + groups)
    branch_rows = in_rows + bwidth
    trunk_lead = feats + classes
    all_scen = scens * scen_rows
    inv_root = 1.0 / math.sqrt(WIDE)
    inv_pairs = 1.0 / math.sqrt(pairs)
    trunk_dests = [
        d for d in range(cells) if ((d + 1) * scens) * own_rows > branch_rows
    ]
    tile = 128
    piece = 32
    pieces = pad_rows // piece
    branch_cells = -(-branch_rows // (scens * own_rows))

    def kernel(hydro, group_h, feat, klass_h, b_in, g_tab, b_out_h, t_in, c_tab, t_out_h,
               targets_h, out,
               group, klass, b_out, t_out, targets, in_sem, x_all, w_b, w_t, x_t, dgelu, hid, coeff, hid_t, dtanh, basis, resid, part_f, part_b,
               part_in, dc, dbasis, dpre_t, pick_t, pick_x, pick_in0, pick_in1, pick_hid, t_own, t_send, t_recv, t_mid, t_relay,
               dpre_b, total,
               x_ss, x_rs, i_ss, i_rs, r_ss, r_rs, p_ss, p_rs, z_ss, z_rs, f_ss, f_rs, n_ss, n_rs, g_ss, g_rs, t_ss, t_rs, m_rs):
        c = lax.axis_index("cell")
        s = lax.axis_index("scen")
        first = (c * scens + s) * own_rows

        def scen_at(k):
            return lax.rem(s + k, scens)

        def cell_at(k):
            return lax.rem(c + k, cells)

        sibling = s + 1 - 2 * lax.rem(s, 2)
        far = lax.rem(s + scens // 2, scens)

        def to_peer(ref, ss, rs, at, peer):
            return pltpu.make_async_remote_copy(
                src_ref=ref, dst_ref=ref, send_sem=ss.at[at], recv_sem=rs.at[at],
                device_id={"scen": peer}, device_id_type=MESH)

        def to_scen(src, dst, ss, rs, k):
            return pltpu.make_async_remote_copy(
                src_ref=src, dst_ref=dst, send_sem=ss.at[k - 1], recv_sem=rs.at[k - 1],
                device_id={"scen": scen_at(k)}, device_id_type=MESH)

        def to_cell(src, dst, ss, rs, k):
            return pltpu.make_async_remote_copy(
                src_ref=src, dst_ref=dst, send_sem=ss.at[k - 1], recv_sem=rs.at[k - 1],
                device_id={"cell": cell_at(k)}, device_id_type=MESH)

        loads = [
            pltpu.make_async_copy(src, dst, in_sem.at[at])
            for at, (src, dst) in enumerate([
                (group_h, group.at[s]),
                (hydro, x_all.at[s, :, 0:samples]),
                (b_in, w_b.at[0:samples]),
                (g_tab, w_b.at[samples:samples + groups]),
                (b_out_h, b_out),
                (feat, x_t.at[:, 0:feats]),
                (klass_h, klass),
                (t_in, w_t.at[0:feats]),
                (c_tab, w_t.at[feats:feats + classes]),
                (t_out_h, t_out),
                (targets_h, targets),
            ])
        ]
        for load in loads:
            load.start()
        barrier = pltpu.get_barrier_semaphore()
        for k in range(1, scens):
            pl.semaphore_signal(barrier, inc=1, device_id={"scen": scen_at(k)}, device_id_type=MESH)
        for k in range(1, cells):
            pl.semaphore_signal(barrier, inc=1, device_id={"cell": cell_at(k)}, device_id_type=MESH)

        pl.semaphore_wait(barrier, scens + cells - 2)
        x_copies = [to_scen(hydro, x_all.at[s, :, 0:samples], x_ss, x_rs, k)
                    for k in range(1, scens)]
        x_copies += [to_scen(group_h, group.at[s], i_ss, i_rs, k) for k in range(1, scens)]
        for copy in x_copies:
            copy.start()

        w_b[samples + groups:, :] = jnp.zeros((128 - groups, bwidth), BF16)
        w_t[feats + classes:, :] = jnp.zeros((128 - classes, twidth), BF16)

        def branch(p):
            hot = (lax.broadcasted_iota(jnp.int32, (128, scen_rows), 0) == group[p]).astype(F32)
            x_all[p, :, samples:samples + 128] = hot.T.astype(BF16)
            pre = contract(x_all[p], w_b[...], 1, 0)
            inner = math.sqrt(2.0 / math.pi)
            bent = jnp.tanh(inner * (pre + 0.044715 * (pre * pre * pre)))
            cdf = 0.5 * (1.0 + bent)
            hid[p] = (pre * cdf).astype(BF16)
            dgelu[p] = cdf + (0.5 * inner) * pre * (1.0 - bent * bent) * (
                1.0 + (3.0 * 0.044715) * (pre * pre))
            coeff[p] = contract(hid[p], b_out[...], 1, 0).astype(BF16)

        for load in loads[0:5]:
            load.wait()
        branch(s)
        for load in loads[5:10]:
            load.wait()

        @pl.loop(0, cell_rows // tile)
        def _(b):
            rows = pl.ds(pl.multiple_of(b * tile, tile), tile)
            lane = lax.broadcasted_iota(jnp.int32, (tile, 128), 1)
            x_t[rows, feats:feats + 128] = (lane == klass[b]).astype(F32).astype(BF16)
            pre = contract(x_t[rows, :], w_t[...], 1, 0)
            bent = jnp.tanh(pre)
            hid_t[rows, :] = bent.astype(BF16)
            dtanh[rows, :] = 1.0 - bent * bent
            basis[rows, :] = contract(hid_t[rows, :], t_out[...], 1, 0).astype(BF16)

        loads[10].wait()
        predicted = contract(coeff[s], basis[...], 1, 1) * inv_root
        resid[s] = ((predicted - targets[...]) * inv_pairs).astype(BF16)
        r_far = to_peer(resid.at[s], r_ss, r_rs, 0, far)
        r_far.start()
        r_near = to_peer(resid.at[s], r_ss, r_rs, 1, sibling)
        r_near.start()
        partial = contract(resid[s], basis[...], 1, 0)
        for d in range(cells):
            part_f[d] = partial[d * chunk:(d + 1) * chunk]
            part_b[d] = partial[d * chunk:(d + 1) * chunk].astype(BF16)
        p_copies = [to_cell(part_b.at[cell_at(k)], part_in.at[k - 1], p_ss, p_rs, k)
                    for k in range(1, cells)]
        for copy in p_copies:
            copy.start()

        def trunk_need(d, me):
            return (d * scens + me + 1) * own_rows > branch_rows

        def lead_need(d, me):
            return ((d * scens + me + 1) * own_rows > branch_rows) & (
                (d * scens + me) * own_rows < branch_rows + trunk_lead)

        lead_any = lead_need(trunk_dests[0], s)
        for d in trunk_dests[1:]:
            lead_any = lead_any | lead_need(d, s)

        for at, d in enumerate(trunk_dests):
            base = (d * scens + s) * own_rows

            @pl.when(trunk_need(d, s))
            def _():
                pick_t[at] = contract(
                    choose(pad_rows, twidth, base, 1, branch_rows + trunk_lead), hid_t[...], 1, 1
                ).astype(BF16)

            @pl.when(lead_need(d, s))
            def _():
                keep = (lax.broadcasted_iota(jnp.int32, (pad_rows, feats + 128), 1)
                        < trunk_lead).astype(F32).astype(BF16)
                pick_x[at] = contract(choose(pad_rows, feats + 128, base, 1, branch_rows) * keep,
                                      x_t[...], 1, 1).astype(BF16)

        for copy in x_copies:
            copy.wait()
        @pl.loop(1, scens)
        def _(k):
            branch(lax.rem(s + k, scens))

        has_in = first < in_rows
        has_hid = (first + own_rows > in_rows) & (first < branch_rows)
        has_trunk = first + own_rows > branch_rows
        x_whole = x_all.reshape(all_scen, samples + 128)
        hid_whole = hid.reshape(all_scen, bwidth)

        @pl.when(has_in)
        def _():
            keep = (lax.broadcasted_iota(jnp.int32, (pad_rows, samples + 128), 1)
                    < samples + groups).astype(F32).astype(BF16)
            pick_in0[...] = contract(choose(pad_rows, samples + 128, first, 2, 0) * keep,
                                     x_whole[...], 1, 1).astype(BF16)
            pick_in1[...] = contract(choose(pad_rows, samples + 128, first, 2, 1) * keep,
                                     x_whole[...], 1, 1).astype(BF16)

        @pl.when(has_hid)
        def _():
            pick_hid[...] = contract(choose(pad_rows, bwidth, first, 1, in_rows),
                                     hid_whole[...], 1, 1).astype(BF16)

        r_far.wait()
        r_pass = to_peer(resid.at[far], r_ss, r_rs, 2, sibling)
        r_pass.start()
        for copy in p_copies:
            copy.wait()
        summed = part_f[c]
        for k in range(cells - 1):
            summed = summed + part_in[k].astype(F32)
        dc[s, c] = summed.astype(BF16)
        z_copies = [to_cell(dc.at[s, c], dc.at[s, c], z_ss, z_rs, k) for k in range(1, cells)]
        takes_dc = c < branch_cells

        def share(j):
            chunk_at = dc.at[s, lax.rem(c + cells - j, cells)]
            return [to_peer(chunk_at, f_ss, f_rs, j, far), to_peer(chunk_at, n_ss, n_rs, j, sibling)]

        def pass_on(j):
            return to_peer(dc.at[far, lax.rem(c + cells - j, cells)], g_ss, g_rs, j, sibling)

        for k, copy in enumerate(z_copies):
            @pl.when(cell_at(k + 1) < branch_cells)
            def _():
                copy.start()

        @pl.when(takes_dc)
        def _():
            for copy in share(0):
                copy.start()

        r_near.wait()
        r_pass.wait()
        @pl.loop(0, cell_rows // tile)
        def _(b):
            cols = pl.ds(pl.multiple_of(b * tile, tile), tile)
            sums = jnp.zeros((tile, WIDE), F32)
            for p in range(scens):
                sums = sums + contract(resid[p, :, cols], coeff[p], 0, 0)
            dbasis[cols, :] = sums.astype(BF16)

        @pl.when(lead_any)
        def _():
            @pl.loop(0, cell_rows // tile)
            def _(b):
                rows = pl.ds(pl.multiple_of(b * tile, tile), tile)
                d_hid = contract(dbasis[rows, :], t_out[...], 1, 1)
                dpre_t[rows, :] = (dtanh[rows, :] * d_hid).astype(BF16)

        def rows_of(j):
            return pl.ds(j * piece, piece)

        def t_copy(at, d, relay, j):
            return pltpu.make_async_remote_copy(
                src_ref=t_send.at[at, rows_of(j)], dst_ref=t_recv.at[relay, rows_of(j)],
                send_sem=t_ss.at[at, j], recv_sem=t_rs.at[relay, j], device_id={"cell": d},
                device_id_type=MESH)

        def m_copy(at, j):
            return pltpu.make_async_remote_copy(
                src_ref=t_send.at[at, rows_of(j)], dst_ref=t_mid.at[at, rows_of(j)],
                send_sem=t_ss.at[at, j], recv_sem=m_rs.at[at, j], device_id={"cell": 1},
                device_id_type=MESH)

        def piece_need(d, j):
            return (d * scens + s) * own_rows + min((j + 1) * piece, own_rows) > branch_rows

        for at, d in reversed(list(enumerate(trunk_dests))):
            @pl.when(trunk_need(d, s))
            def _():
                total[...] = contract(pick_t[at], dbasis[...], 1, 0)

                @pl.when(lead_need(d, s))
                def _():
                    total[...] += contract(pick_x[at], dpre_t[...], 1, 0)

                @pl.when(c == d)
                def _():
                    t_own[...] = total[...]

                @pl.when(c == 1)
                def _():
                    t_relay[at] = total[...]

                @pl.when((c != d) & (c != 1))
                def _():
                    t_send[at] = total[...].astype(BF16)

                for j in range(pieces):
                    @pl.when((c != d) & (c > 1) & piece_need(d, j))
                    def _():
                        t_copy(at, d, 0, j).start()

                    @pl.when((c == 0) & piece_need(d, j))
                    def _():
                        m_copy(at, j).start()

        for k, copy in enumerate(z_copies):
            @pl.when(takes_dc)
            def _():
                copy.wait_recv()
                for other in share(k + 1):
                    other.start()

        for j in range(cells):
            @pl.when(takes_dc)
            def _():
                share(j)[0].wait_recv()
                pass_on(j).start()

        for at, d in reversed(list(enumerate(trunk_dests))):
            for j in range(pieces):
                @pl.when((c == 1) & piece_need(d, j))
                def _():
                    m_copy(at, j).wait_recv()
                    t_send[at, rows_of(j)] = (
                        t_relay[at, rows_of(j)] + t_mid[at, rows_of(j)].astype(F32)).astype(BF16)
                    t_copy(at, d, 1, j).start()

        dc_rows = dc.reshape(scens, scen_rows, WIDE)

        def through_gelu(p):
            @pl.when(has_in)
            def _():
                d_hid = contract(dc_rows[p], b_out[...], 1, 1)
                rows = pl.ds(pl.multiple_of(p * scen_rows, scen_rows), scen_rows)
                dpre_b[rows, :] = (d_hid * dgelu[p]).astype(BF16)

        total[...] = jnp.zeros_like(total)
        through_gelu(s)
        through_gelu(far)

        @pl.when(takes_dc)
        def _():
            for j in range(cells):
                share(j)[1].wait_recv()
        through_gelu(sibling)

        @pl.when(takes_dc)
        def _():
            for j in range(cells):
                pass_on(j).wait_recv()
        through_gelu(lax.rem(sibling + scens // 2, scens))
        dc_whole = dc.reshape(all_scen, WIDE)

        @pl.when(has_hid)
        def _():
            total[...] += contract(pick_hid[...], dc_whole[...], 1, 0)

        @pl.when(has_in)
        def _():
            total[...] += contract(pick_in0[...], dpre_b[:, :WIDE], 1, 0)
            total[...] += contract(pick_in1[...], dpre_b[:, WIDE:], 1, 0)

        @pl.when(has_trunk)
        def _():
            total[...] += t_own[...]
            for j in range(pieces):
                @pl.when(first + min((j + 1) * piece, own_rows) > branch_rows)
                def _():
                    for k in range(2):
                        t_copy(0, 0, k, j).wait_recv()
                        total[rows_of(j)] += t_recv[k, rows_of(j)].astype(F32)

        for j in range(WIDE // 128):
            out[pl.ds(j, own_rows, WIDE // 128), :] = total[0:own_rows, j * 128:(j + 1) * 128]

        for k, copy in enumerate(z_copies):
            @pl.when(cell_at(k + 1) < branch_cells)
            def _():
                copy.wait_send()

        @pl.when(takes_dc)
        def _():
            for j in range(cells):
                for copy in share(j) + [pass_on(j)]:
                    copy.wait_send()

        for at, d in enumerate(trunk_dests):
            for j in range(pieces):
                @pl.when((c != d) & piece_need(d, j))
                def _():
                    t_copy(at, d, 0, j).wait_send()

    dma = pltpu.SemaphoreType.DMA
    scratch = [
        pltpu.VMEM((scens, 1, scen_rows), jnp.int32),
        pltpu.SMEM((cell_rows // 128,), jnp.int32),
        pltpu.VMEM((bwidth, WIDE), BF16),
        pltpu.VMEM((twidth, WIDE), BF16),
        pltpu.VMEM((scen_rows, cell_rows), F32),
        dma((11,)),
        pltpu.VMEM((scens, scen_rows, samples + 128), BF16),
        pltpu.VMEM((samples + 128, bwidth), BF16),
        pltpu.VMEM((feats + 128, twidth), BF16),
        pltpu.VMEM((cell_rows, feats + 128), BF16),
        pltpu.VMEM((scens, scen_rows, bwidth), F32),
        pltpu.VMEM((scens, scen_rows, bwidth), BF16),
        pltpu.VMEM((scens, scen_rows, WIDE), BF16),
        pltpu.VMEM((cell_rows, twidth), BF16),
        pltpu.VMEM((cell_rows, twidth), F32),
        pltpu.VMEM((cell_rows, WIDE), BF16),
        pltpu.VMEM((scens, scen_rows, cell_rows), BF16),
        pltpu.VMEM((cells, chunk, WIDE), F32),
        pltpu.VMEM((cells, chunk, WIDE), BF16),
        pltpu.VMEM((cells - 1, chunk, WIDE), BF16),
        pltpu.VMEM((scens, cells, chunk, WIDE), BF16),
        pltpu.VMEM((cell_rows, WIDE), BF16),
        pltpu.VMEM((cell_rows, twidth), BF16),
        pltpu.VMEM((len(trunk_dests), pad_rows, cell_rows), BF16),
        pltpu.VMEM((len(trunk_dests), pad_rows, cell_rows), BF16),
        pltpu.VMEM((pad_rows, all_scen), BF16),
        pltpu.VMEM((pad_rows, all_scen), BF16),
        pltpu.VMEM((pad_rows, all_scen), BF16),
        pltpu.VMEM((pad_rows, WIDE), F32),
        pltpu.VMEM((len(trunk_dests), pad_rows, WIDE), BF16),
        pltpu.VMEM((2, pad_rows, WIDE), BF16),
        pltpu.VMEM((len(trunk_dests), pad_rows, WIDE), BF16),
        pltpu.VMEM((len(trunk_dests), pad_rows, WIDE), F32),
        pltpu.VMEM((all_scen, bwidth), BF16),
        pltpu.VMEM((pad_rows, WIDE), F32),
        dma((scens - 1,)), dma((scens - 1,)),
        dma((scens - 1,)), dma((scens - 1,)),
        dma((scens - 1,)), dma((scens - 1,)),
        dma((cells - 1,)), dma((cells - 1,)),
        dma((cells - 1,)), dma((cells - 1,)),
        dma((cells,)), dma((cells,)),
        dma((cells,)), dma((cells,)),
        dma((cells,)), dma((cells,)),
        dma((len(trunk_dests), pieces)), dma((2, pieces)), dma((len(trunk_dests), pieces)),
    ]
    return kernel, scratch


def shards(hydrograph, scen_group, cell_feat, cell_class, branch_in, group_table, branch_out,
           trunk_in, class_table, trunk_out, targets):
    cells = lax.axis_size("cell")
    scens = lax.axis_size("scen")
    scen_rows, samples = hydrograph.shape
    cell_rows, feats = cell_feat.shape
    bwidth, width = branch_out.shape
    twidth = trunk_in.shape[1]
    groups, classes = group_table.shape[0], class_table.shape[0]
    size = (samples + groups + width) * bwidth + (feats + classes + width) * twidth
    block = size // (cells * scens)
    fits = (
        cells == 4 and scens == 4 and width == WIDE and twidth == WIDE and bwidth == 2 * WIDE
        and block % WIDE == 0 and block * cells * scens == size
        and scen_rows == 128 and scen_rows % (16 * cells) == 0 and cell_rows % 128 == 0
        and samples == 128 and feats == 128 and groups <= 128 and classes <= 128
        and groups % 16 == 0 and classes % 16 == 0 and scens * scen_rows <= 1024
        and cell_rows <= 512 and (samples + groups) * 2 + bwidth >= 2 * scens * (block // WIDE)
    )
    if not fits:
        return plain_shards(hydrograph, scen_group, cell_feat, cell_class, branch_in, group_table,
                            branch_out, trunk_in, class_table, trunk_out, targets)
    pairs = float(scen_rows * scens) * float(cell_rows * cells)
    kernel, scratch = make_kernel(cells, scens, scen_rows, cell_rows, bwidth, twidth, groups,
                                  classes, samples, feats, block // WIDE, pairs)
    vmem = pl.BlockSpec(memory_space=pltpu.VMEM)
    hbm = pl.BlockSpec(memory_space=pltpu.HBM)
    out = pl.pallas_call(
        kernel,
        out_shape=jax.ShapeDtypeStruct((block // 128, 128), F32),
        in_specs=[hbm] * 11,
        out_specs=vmem,
        scratch_shapes=scratch,
        compiler_params=pltpu.CompilerParams(
            collective_id=0, has_side_effects=True, vmem_limit_bytes=64 * 1024 * 1024),
    )(hydrograph, scen_group.reshape(1, scen_rows), cell_feat, cell_class, branch_in, group_table,
      branch_out, trunk_in, class_table, trunk_out, targets)
    return out.reshape(block)


def solution(mesh):
    in_specs = (
        P(("rep", "scen"), None),
        P(("rep", "scen")),
        P(("rep", "cell"), None),
        P(("rep", "cell")),
        P(),
        P(),
        P(),
        P(),
        P(),
        P(),
        P(("rep", "scen"), "cell"),
    )
    out_specs = P(("rep", "cell", "scen"))
    return jax.shard_map(shards, mesh=mesh, in_specs=in_specs, out_specs=out_specs, check_vma=False)
```

```python
import math

import jax
import jax.numpy as jnp
from jax import lax
from jax.experimental import pallas as pl
from jax.experimental.pallas import tpu as pltpu
from jax.sharding import PartitionSpec as P

MESH = pl.DeviceIdType.MESH
BF16 = jnp.bfloat16
F32 = jnp.float32
WIDE = 512


def contract(left, right, left_dim, right_dim):
    return lax.dot_general(
        left, right, (((left_dim,), (right_dim,)), ((), ())), preferred_element_type=jnp.float32
    )


def plain_shards(
    hydrograph,
    scen_group,
    cell_feat,
    cell_class,
    branch_in,
    group_table,
    branch_out,
    trunk_in,
    class_table,
    trunk_out,
    targets,
):
    cell_count = lax.axis_size("cell")
    scen_count = lax.axis_size("scen")
    whole_pairs = jnp.float32(hydrograph.shape[0] * scen_count) * jnp.float32(
        cell_feat.shape[0] * cell_count
    )
    group_hot = (
        scen_group[:, None] == jnp.arange(group_table.shape[0], dtype=jnp.int32)[None, :]
    ).astype(BF16)
    class_cells = jnp.repeat(cell_class, 128)
    class_hot = (
        class_cells[:, None] == jnp.arange(class_table.shape[0], dtype=jnp.int32)[None, :]
    ).astype(BF16)
    pre_branch = contract(hydrograph, branch_in, 1, 0) + contract(group_hot, group_table, 1, 0)
    hid_branch = jax.nn.gelu(pre_branch).astype(BF16)
    coeff_local = contract(hid_branch, branch_out, 1, 0).astype(BF16)
    pre_trunk = contract(cell_feat, trunk_in, 1, 0) + contract(class_hot, class_table, 1, 0)
    hid_trunk = jnp.tanh(pre_trunk).astype(BF16)
    basis_local = contract(hid_trunk, trunk_out, 1, 0).astype(BF16)
    predicted = contract(coeff_local, basis_local, 1, 1) * (
        1.0 / jnp.sqrt(jnp.float32(branch_out.shape[1]))
    )
    resid = ((predicted - targets) * (1.0 / jnp.sqrt(whole_pairs))).astype(BF16)
    d_coeff = lax.psum(contract(resid, basis_local, 1, 0), "cell").astype(BF16)
    d_basis = lax.psum(contract(resid, coeff_local, 0, 0).astype(BF16), "scen")
    g_branch_out = contract(hid_branch, d_coeff, 0, 0)
    d_hid_branch = contract(d_coeff, branch_out, 1, 1)
    d_pre_branch = jax.vjp(jax.nn.gelu, pre_branch)[1](d_hid_branch)[0].astype(BF16)
    g_branch_in = contract(hydrograph, d_pre_branch, 0, 0)
    g_group_table = contract(group_hot, d_pre_branch, 0, 0)
    g_trunk_out = contract(hid_trunk, d_basis, 0, 0)
    d_hid_trunk = contract(d_basis, trunk_out, 1, 1)
    d_pre_trunk = jax.vjp(jnp.tanh, pre_trunk)[1](d_hid_trunk)[0].astype(BF16)
    g_trunk_in = contract(cell_feat, d_pre_trunk, 0, 0)
    g_class_table = contract(class_hot, d_pre_trunk, 0, 0)
    branch_flat = jnp.concatenate(
        [g_branch_in.ravel(), g_group_table.ravel(), g_branch_out.ravel()]
    )
    trunk_flat = jnp.concatenate([g_trunk_in.ravel(), g_class_table.ravel(), g_trunk_out.ravel()])
    branch_flat = branch_flat * (lax.axis_index("cell") == 0).astype(F32)
    trunk_flat = trunk_flat * (lax.axis_index("scen") == 0).astype(F32)
    flat_grad = jnp.concatenate([branch_flat, trunk_flat])
    return lax.psum_scatter(flat_grad, ("cell", "scen"), scatter_dimension=0, tiled=True)


def choose(rows, cols, first, scale, offset):
    row = lax.broadcasted_iota(jnp.int32, (rows, cols), 0) + first
    col = lax.broadcasted_iota(jnp.int32, (rows, cols), 1) * scale + offset
    return (row == col).astype(F32).astype(BF16)


def make_kernel(cells, scens, scen_rows, cell_rows, bwidth, twidth, groups, classes, samples, feats,
                own_rows, pairs):
    pad_rows = -(-own_rows // 32) * 32
    chunk = scen_rows // cells
    in_rows = 2 * (samples + groups)
    branch_rows = in_rows + bwidth
    trunk_lead = feats + classes
    all_scen = scens * scen_rows
    inv_root = 1.0 / math.sqrt(WIDE)
    inv_pairs = 1.0 / math.sqrt(pairs)
    trunk_dests = [
        d for d in range(cells) if ((d + 1) * scens) * own_rows > branch_rows
    ]
    tile = 128
    piece = 32
    pieces = pad_rows // piece
    branch_cells = -(-branch_rows // (scens * own_rows))

    def kernel(hydro, group_h, feat, klass_h, b_in, g_tab, b_out_h, t_in, c_tab, t_out_h,
               targets_h, out,
               group, klass, b_out, t_out, targets, in_sem, x_all, w_b, w_t, x_t, dgelu, hid, coeff, hid_t, dtanh, basis, resid, part_f, part_b,
               part_in, dc, dbasis, dpre_t, pick_t, pick_x, pick_in0, pick_in1, pick_hid, t_own, t_send, t_recv, t_mid, t_relay,
               dpre_b, total,
               x_ss, x_rs, i_ss, i_rs, r_ss, r_rs, p_ss, p_rs, z_ss, z_rs, f_ss, f_rs, n_ss, n_rs, g_ss, g_rs, t_ss, t_rs, m_rs):
        c = lax.axis_index("cell")
        s = lax.axis_index("scen")
        first = (c * scens + s) * own_rows

        def scen_at(k):
            return lax.rem(s + k, scens)

        def cell_at(k):
            return lax.rem(c + k, cells)

        sibling = s + 1 - 2 * lax.rem(s, 2)
        far = lax.rem(s + scens // 2, scens)

        def to_peer(ref, ss, rs, at, peer):
            return pltpu.make_async_remote_copy(
                src_ref=ref, dst_ref=ref, send_sem=ss.at[at], recv_sem=rs.at[at],
                device_id={"scen": peer}, device_id_type=MESH)

        def to_scen(src, dst, ss, rs, k):
            return pltpu.make_async_remote_copy(
                src_ref=src, dst_ref=dst, send_sem=ss.at[k - 1], recv_sem=rs.at[k - 1],
                device_id={"scen": scen_at(k)}, device_id_type=MESH)

        def to_cell(src, dst, ss, rs, k):
            return pltpu.make_async_remote_copy(
                src_ref=src, dst_ref=dst, send_sem=ss.at[k - 1], recv_sem=rs.at[k - 1],
                device_id={"cell": cell_at(k)}, device_id_type=MESH)

        loads = [
            pltpu.make_async_copy(src, dst, in_sem.at[at])
            for at, (src, dst) in enumerate([
                (group_h, group.at[s]),
                (hydro, x_all.at[s, :, 0:samples]),
                (b_in, w_b.at[0:samples]),
                (g_tab, w_b.at[samples:samples + groups]),
                (b_out_h, b_out),
                (feat, x_t.at[:, 0:feats]),
                (klass_h, klass),
                (t_in, w_t.at[0:feats]),
                (c_tab, w_t.at[feats:feats + classes]),
                (t_out_h, t_out),
                (targets_h, targets),
            ])
        ]
        for load in loads:
            load.start()
        barrier = pltpu.get_barrier_semaphore()
        for k in range(1, scens):
            pl.semaphore_signal(barrier, inc=1, device_id={"scen": scen_at(k)}, device_id_type=MESH)
        for k in range(1, cells):
            pl.semaphore_signal(barrier, inc=1, device_id={"cell": cell_at(k)}, device_id_type=MESH)

        pl.semaphore_wait(barrier, scens + cells - 2)
        x_copies = [to_scen(hydro, x_all.at[s, :, 0:samples], x_ss, x_rs, k)
                    for k in range(1, scens)]
        x_copies += [to_scen(group_h, group.at[s], i_ss, i_rs, k) for k in range(1, scens)]
        for copy in x_copies:
            copy.start()

        w_b[samples + groups:, :] = jnp.zeros((128 - groups, bwidth), BF16)
        w_t[feats + classes:, :] = jnp.zeros((128 - classes, twidth), BF16)

        def branch(p):
            hot = (lax.broadcasted_iota(jnp.int32, (128, scen_rows), 0) == group[p]).astype(F32)
            x_all[p, :, samples:samples + 128] = hot.T.astype(BF16)
            pre = contract(x_all[p], w_b[...], 1, 0)
            inner = math.sqrt(2.0 / math.pi)
            bent = jnp.tanh(inner * (pre + 0.044715 * (pre * pre * pre)))
            cdf = 0.5 * (1.0 + bent)
            hid[p] = (pre * cdf).astype(BF16)
            dgelu[p] = cdf + (0.5 * inner) * pre * (1.0 - bent * bent) * (
                1.0 + (3.0 * 0.044715) * (pre * pre))
            coeff[p] = contract(hid[p], b_out[...], 1, 0).astype(BF16)

        for load in loads[0:5]:
            load.wait()
        branch(s)
        for load in loads[5:10]:
            load.wait()

        @pl.loop(0, cell_rows // tile)
        def _(b):
            rows = pl.ds(pl.multiple_of(b * tile, tile), tile)
            lane = lax.broadcasted_iota(jnp.int32, (tile, 128), 1)
            x_t[rows, feats:feats + 128] = (lane == klass[b]).astype(F32).astype(BF16)
            pre = contract(x_t[rows, :], w_t[...], 1, 0)
            bent = jnp.tanh(pre)
            hid_t[rows, :] = bent.astype(BF16)
            dtanh[rows, :] = 1.0 - bent * bent
            basis[rows, :] = contract(hid_t[rows, :], t_out[...], 1, 0).astype(BF16)

        loads[10].wait()
        predicted = contract(coeff[s], basis[...], 1, 1) * inv_root
        resid[s] = ((predicted - targets[...]) * inv_pairs).astype(BF16)
        r_far = to_peer(resid.at[s], r_ss, r_rs, 0, far)
        r_far.start()
        r_near = to_peer(resid.at[s], r_ss, r_rs, 1, sibling)
        r_near.start()
        partial = contract(resid[s], basis[...], 1, 0)
        for d in range(cells):
            part_f[d] = partial[d * chunk:(d + 1) * chunk]
            part_b[d] = partial[d * chunk:(d + 1) * chunk].astype(BF16)
        p_copies = [to_cell(part_b.at[cell_at(k)], part_in.at[k - 1], p_ss, p_rs, k)
                    for k in range(1, cells)]
        for copy in p_copies:
            copy.start()

        def trunk_need(d, me):
            return (d * scens + me + 1) * own_rows > branch_rows

        def lead_need(d, me):
            return ((d * scens + me + 1) * own_rows > branch_rows) & (
                (d * scens + me) * own_rows < branch_rows + trunk_lead)

        lead_any = lead_need(trunk_dests[0], s)
        for d in trunk_dests[1:]:
            lead_any = lead_any | lead_need(d, s)

        for at, d in enumerate(trunk_dests):
            base = (d * scens + s) * own_rows

            @pl.when(trunk_need(d, s))
            def _():
                pick_t[at] = contract(
                    choose(pad_rows, twidth, base, 1, branch_rows + trunk_lead), hid_t[...], 1, 1
                ).astype(BF16)

            @pl.when(lead_need(d, s))
            def _():
                keep = (lax.broadcasted_iota(jnp.int32, (pad_rows, feats + 128), 1)
                        < trunk_lead).astype(F32).astype(BF16)
                pick_x[at] = contract(choose(pad_rows, feats + 128, base, 1, branch_rows) * keep,
                                      x_t[...], 1, 1).astype(BF16)

        for copy in x_copies:
            copy.wait()
        @pl.loop(1, scens)
        def _(k):
            branch(lax.rem(s + k, scens))

        r_far.wait()
        r_pass = to_peer(resid.at[far], r_ss, r_rs, 2, sibling)
        r_pass.start()
        for copy in p_copies:
            copy.wait()
        summed = part_f[c]
        for k in range(cells - 1):
            summed = summed + part_in[k].astype(F32)
        dc[s, c] = summed.astype(BF16)
        z_copies = [to_cell(dc.at[s, c], dc.at[s, c], z_ss, z_rs, k) for k in range(1, cells)]
        takes_dc = c < branch_cells

        def share(j):
            chunk_at = dc.at[s, lax.rem(c + cells - j, cells)]
            return [to_peer(chunk_at, f_ss, f_rs, j, far), to_peer(chunk_at, n_ss, n_rs, j, sibling)]

        def pass_on(j):
            return to_peer(dc.at[far, lax.rem(c + cells - j, cells)], g_ss, g_rs, j, sibling)

        for k, copy in enumerate(z_copies):
            @pl.when(cell_at(k + 1) < branch_cells)
            def _():
                copy.start()

        @pl.when(takes_dc)
        def _():
            for copy in share(0):
                copy.start()

        has_in = first < in_rows
        has_hid = (first + own_rows > in_rows) & (first < branch_rows)
        has_trunk = first + own_rows > branch_rows
        x_whole = x_all.reshape(all_scen, samples + 128)
        hid_whole = hid.reshape(all_scen, bwidth)

        @pl.when(has_in)
        def _():
            keep = (lax.broadcasted_iota(jnp.int32, (pad_rows, samples + 128), 1)
                    < samples + groups).astype(F32).astype(BF16)
            pick_in0[...] = contract(choose(pad_rows, samples + 128, first, 2, 0) * keep,
                                     x_whole[...], 1, 1).astype(BF16)
            pick_in1[...] = contract(choose(pad_rows, samples + 128, first, 2, 1) * keep,
                                     x_whole[...], 1, 1).astype(BF16)

        @pl.when(has_hid)
        def _():
            pick_hid[...] = contract(choose(pad_rows, bwidth, first, 1, in_rows),
                                     hid_whole[...], 1, 1).astype(BF16)

        r_near.wait()
        r_pass.wait()
        @pl.loop(0, cell_rows // tile)
        def _(b):
            cols = pl.ds(pl.multiple_of(b * tile, tile), tile)
            sums = jnp.zeros((tile, WIDE), F32)
            for p in range(scens):
                sums = sums + contract(resid[p, :, cols], coeff[p], 0, 0)
            dbasis[cols, :] = sums.astype(BF16)

        @pl.when(lead_any)
        def _():
            @pl.loop(0, cell_rows // tile)
            def _(b):
                rows = pl.ds(pl.multiple_of(b * tile, tile), tile)
                d_hid = contract(dbasis[rows, :], t_out[...], 1, 1)
                dpre_t[rows, :] = (dtanh[rows, :] * d_hid).astype(BF16)

        def rows_of(j):
            return pl.ds(j * piece, piece)

        def t_copy(at, d, relay, j):
            return pltpu.make_async_remote_copy(
                src_ref=t_send.at[at, rows_of(j)], dst_ref=t_recv.at[relay, rows_of(j)],
                send_sem=t_ss.at[at, j], recv_sem=t_rs.at[relay, j], device_id={"cell": d},
                device_id_type=MESH)

        def m_copy(at, j):
            return pltpu.make_async_remote_copy(
                src_ref=t_send.at[at, rows_of(j)], dst_ref=t_mid.at[at, rows_of(j)],
                send_sem=t_ss.at[at, j], recv_sem=m_rs.at[at, j], device_id={"cell": 1},
                device_id_type=MESH)

        def piece_need(d, j):
            return (d * scens + s) * own_rows + min((j + 1) * piece, own_rows) > branch_rows

        for at, d in reversed(list(enumerate(trunk_dests))):
            @pl.when(trunk_need(d, s))
            def _():
                total[...] = contract(pick_t[at], dbasis[...], 1, 0)

                @pl.when(lead_need(d, s))
                def _():
                    total[...] += contract(pick_x[at], dpre_t[...], 1, 0)

                @pl.when(c == d)
                def _():
                    t_own[...] = total[...]

                @pl.when(c == 1)
                def _():
                    t_relay[at] = total[...]

                @pl.when((c != d) & (c != 1))
                def _():
                    t_send[at] = total[...].astype(BF16)

                for j in range(pieces):
                    @pl.when((c != d) & (c > 1) & piece_need(d, j))
                    def _():
                        t_copy(at, d, 0, j).start()

                    @pl.when((c == 0) & piece_need(d, j))
                    def _():
                        m_copy(at, j).start()

        for k, copy in enumerate(z_copies):
            @pl.when(takes_dc)
            def _():
                copy.wait_recv()
                for other in share(k + 1):
                    other.start()

        for j in range(cells):
            @pl.when(takes_dc)
            def _():
                share(j)[0].wait_recv()
                pass_on(j).start()

        for at, d in reversed(list(enumerate(trunk_dests))):
            for j in range(pieces):
                @pl.when((c == 1) & piece_need(d, j))
                def _():
                    m_copy(at, j).wait_recv()
                    t_send[at, rows_of(j)] = (
                        t_relay[at, rows_of(j)] + t_mid[at, rows_of(j)].astype(F32)).astype(BF16)
                    t_copy(at, d, 1, j).start()

        dc_rows = dc.reshape(scens, scen_rows, WIDE)

        def through_gelu(p):
            @pl.when(has_in)
            def _():
                d_hid = contract(dc_rows[p], b_out[...], 1, 1)
                rows = pl.ds(pl.multiple_of(p * scen_rows, scen_rows), scen_rows)
                dpre_b[rows, :] = (d_hid * dgelu[p]).astype(BF16)

        total[...] = jnp.zeros_like(total)
        through_gelu(s)
        through_gelu(far)

        @pl.when(takes_dc)
        def _():
            for j in range(cells):
                share(j)[1].wait_recv()
        through_gelu(sibling)

        @pl.when(takes_dc)
        def _():
            for j in range(cells):
                pass_on(j).wait_recv()
        through_gelu(lax.rem(sibling + scens // 2, scens))
        dc_whole = dc.reshape(all_scen, WIDE)

        @pl.when(has_hid)
        def _():
            total[...] += contract(pick_hid[...], dc_whole[...], 1, 0)

        @pl.when(has_in)
        def _():
            total[...] += contract(pick_in0[...], dpre_b[:, :WIDE], 1, 0)
            total[...] += contract(pick_in1[...], dpre_b[:, WIDE:], 1, 0)

        @pl.when(has_trunk)
        def _():
            total[...] += t_own[...]
            for j in range(pieces):
                @pl.when(first + min((j + 1) * piece, own_rows) > branch_rows)
                def _():
                    for k in range(2):
                        t_copy(0, 0, k, j).wait_recv()
                        total[rows_of(j)] += t_recv[k, rows_of(j)].astype(F32)

        for j in range(WIDE // 128):
            out[pl.ds(j, own_rows, WIDE // 128), :] = total[0:own_rows, j * 128:(j + 1) * 128]

        for k, copy in enumerate(z_copies):
            @pl.when(cell_at(k + 1) < branch_cells)
            def _():
                copy.wait_send()

        @pl.when(takes_dc)
        def _():
            for j in range(cells):
                for copy in share(j) + [pass_on(j)]:
                    copy.wait_send()

        for at, d in enumerate(trunk_dests):
            for j in range(pieces):
                @pl.when((c != d) & piece_need(d, j))
                def _():
                    t_copy(at, d, 0, j).wait_send()

    dma = pltpu.SemaphoreType.DMA
    scratch = [
        pltpu.VMEM((scens, 1, scen_rows), jnp.int32),
        pltpu.SMEM((cell_rows // 128,), jnp.int32),
        pltpu.VMEM((bwidth, WIDE), BF16),
        pltpu.VMEM((twidth, WIDE), BF16),
        pltpu.VMEM((scen_rows, cell_rows), F32),
        dma((11,)),
        pltpu.VMEM((scens, scen_rows, samples + 128), BF16),
        pltpu.VMEM((samples + 128, bwidth), BF16),
        pltpu.VMEM((feats + 128, twidth), BF16),
        pltpu.VMEM((cell_rows, feats + 128), BF16),
        pltpu.VMEM((scens, scen_rows, bwidth), F32),
        pltpu.VMEM((scens, scen_rows, bwidth), BF16),
        pltpu.VMEM((scens, scen_rows, WIDE), BF16),
        pltpu.VMEM((cell_rows, twidth), BF16),
        pltpu.VMEM((cell_rows, twidth), F32),
        pltpu.VMEM((cell_rows, WIDE), BF16),
        pltpu.VMEM((scens, scen_rows, cell_rows), BF16),
        pltpu.VMEM((cells, chunk, WIDE), F32),
        pltpu.VMEM((cells, chunk, WIDE), BF16),
        pltpu.VMEM((cells - 1, chunk, WIDE), BF16),
        pltpu.VMEM((scens, cells, chunk, WIDE), BF16),
        pltpu.VMEM((cell_rows, WIDE), BF16),
        pltpu.VMEM((cell_rows, twidth), BF16),
        pltpu.VMEM((len(trunk_dests), pad_rows, cell_rows), BF16),
        pltpu.VMEM((len(trunk_dests), pad_rows, cell_rows), BF16),
        pltpu.VMEM((pad_rows, all_scen), BF16),
        pltpu.VMEM((pad_rows, all_scen), BF16),
        pltpu.VMEM((pad_rows, all_scen), BF16),
        pltpu.VMEM((pad_rows, WIDE), F32),
        pltpu.VMEM((len(trunk_dests), pad_rows, WIDE), BF16),
        pltpu.VMEM((2, pad_rows, WIDE), BF16),
        pltpu.VMEM((len(trunk_dests), pad_rows, WIDE), BF16),
        pltpu.VMEM((len(trunk_dests), pad_rows, WIDE), F32),
        pltpu.VMEM((all_scen, bwidth), BF16),
        pltpu.VMEM((pad_rows, WIDE), F32),
        dma((scens - 1,)), dma((scens - 1,)),
        dma((scens - 1,)), dma((scens - 1,)),
        dma((scens - 1,)), dma((scens - 1,)),
        dma((cells - 1,)), dma((cells - 1,)),
        dma((cells - 1,)), dma((cells - 1,)),
        dma((cells,)), dma((cells,)),
        dma((cells,)), dma((cells,)),
        dma((cells,)), dma((cells,)),
        dma((len(trunk_dests), pieces)), dma((2, pieces)), dma((len(trunk_dests), pieces)),
    ]
    return kernel, scratch


def shards(hydrograph, scen_group, cell_feat, cell_class, branch_in, group_table, branch_out,
           trunk_in, class_table, trunk_out, targets):
    cells = lax.axis_size("cell")
    scens = lax.axis_size("scen")
    scen_rows, samples = hydrograph.shape
    cell_rows, feats = cell_feat.shape
    bwidth, width = branch_out.shape
    twidth = trunk_in.shape[1]
    groups, classes = group_table.shape[0], class_table.shape[0]
    size = (samples + groups + width) * bwidth + (feats + classes + width) * twidth
    block = size // (cells * scens)
    fits = (
        cells == 4 and scens == 4 and width == WIDE and twidth == WIDE and bwidth == 2 * WIDE
        and block % WIDE == 0 and block * cells * scens == size
        and scen_rows == 128 and scen_rows % (16 * cells) == 0 and cell_rows % 128 == 0
        and samples == 128 and feats == 128 and groups <= 128 and classes <= 128
        and groups % 16 == 0 and classes % 16 == 0 and scens * scen_rows <= 1024
        and cell_rows <= 512 and (samples + groups) * 2 + bwidth >= 2 * scens * (block // WIDE)
    )
    if not fits:
        return plain_shards(hydrograph, scen_group, cell_feat, cell_class, branch_in, group_table,
                            branch_out, trunk_in, class_table, trunk_out, targets)
    pairs = float(scen_rows * scens) * float(cell_rows * cells)
    kernel, scratch = make_kernel(cells, scens, scen_rows, cell_rows, bwidth, twidth, groups,
                                  classes, samples, feats, block // WIDE, pairs)
    vmem = pl.BlockSpec(memory_space=pltpu.VMEM)
    hbm = pl.BlockSpec(memory_space=pltpu.HBM)
    out = pl.pallas_call(
        kernel,
        out_shape=jax.ShapeDtypeStruct((block // 128, 128), F32),
        in_specs=[hbm] * 11,
        out_specs=vmem,
        scratch_shapes=scratch,
        compiler_params=pltpu.CompilerParams(
            collective_id=0, has_side_effects=True, vmem_limit_bytes=64 * 1024 * 1024),
    )(hydrograph, scen_group.reshape(1, scen_rows), cell_feat, cell_class, branch_in, group_table,
      branch_out, trunk_in, class_table, trunk_out, targets)
    return out.reshape(block)


def solution(mesh):
    in_specs = (
        P(("rep", "scen"), None),
        P(("rep", "scen")),
        P(("rep", "cell"), None),
        P(("rep", "cell")),
        P(),
        P(),
        P(),
        P(),
        P(),
        P(),
        P(("rep", "scen"), "cell"),
    )
    out_specs = P(("rep", "cell", "scen"))
    return jax.shard_map(shards, mesh=mesh, in_specs=in_specs, out_specs=out_specs, check_vma=False)
```
